128 devices in a mesh: node: 16 (over z, y_hi, core), local: 8 (over y_lo, x).
Axes of the slice: x: 4, y: 4 (y_hi: 2, y_lo: 2; y = y_hi * 2 + y_lo), z: 4, core: 2. Of those that a mesh axis runs over, the one named last changes fastest.
Arguments:
- tokens: bfloat16 [32768, 14336], P(('node', 'local')), may hold values from -24 to 24
- cotangent: bfloat16 [32768, 384], P(('node', 'local')), may hold values from -12 to 12
- master: float32 [384, 14336], P('local', 'node'), may hold values from -0.046875 to 0.046875
- moment_one: float32 [384, 14336], P('local', 'node'), may hold values from -6 to 6
- moment_two: float32 [384, 14336], P('local', 'node'), may hold values from 0.5 to 8
Outputs:
- hidden: bfloat16 [32768, 384], P(('node', 'local'))
- input_grad: bfloat16 [32768, 14336], P(('node', 'local'))
- gradient: float32 [384, 14336], P('local', 'node')
- master_new: float32 [384, 14336], P('local', 'node')
- moment_one_new: float32 [384, 14336], P('local', 'node')
- moment_two_new: float32 [384, 14336], P('local', 'node')
The draws below stay inside these ranges and needn't reach their ends.
All inputs are finite; a program needn't handle non-finite values.
Results may differ from the reference program's by a relative error of at most 0.022.
Values may be sent and summed in bfloat16 or wider, within the bound.
A program may use at most 128 MiB of HBM per device.

```python
import math
import jax
import jax.numpy as jnp
from jax import lax

D = 14336
TOK_DEV = 256
STEP = 10
FF = 384
TOKENS = 32768
DEVICES = 128


def with_spikes(values, stream_key, source, target, shards_of, factor):
    owner, partner = [(jnp.arange(values.shape[axis_at]) // (values.shape[axis_at] // shards_of)).reshape([-1 if axis == axis_at else 1 for axis in range(values.ndim)]) for axis_at in (source, target)]
    chosen = jax.random.permutation(stream_key, shards_of)[partner]
    strong = (owner == chosen) | (owner == (partner + shards_of // 2) % shards_of)
    return jnp.where(strong, factor * values, values)


def block_levels(key, dims, pieces, smallest, high):
    level, own = 1.0, jax.random.fold_in(key, 6)
    for axis_at, shards_of in pieces:
        heights = jnp.exp(jax.random.uniform(jax.random.fold_in(own, axis_at), (shards_of,), jnp.float32, smallest / len(pieces), high / len(pieces)))
        level = level * jnp.repeat(heights, dims[axis_at] // shards_of).reshape([-1 if axis == axis_at else 1 for axis in range(len(dims))])
    return level


def gaussian(stream_key, extent, spread, most, split=(), dtype=jnp.bfloat16):
    gain = block_levels(stream_key, extent, split, -0.22, 0.18) if split else 1.0
    drawn = jax.random.normal(stream_key, extent, jnp.float32) * spread * gain
    return jnp.minimum(jnp.maximum(drawn, -most), most).astype(dtype)


def heavy_noise(rng, shape, spread, reach, pieces, heavy, dtype=jnp.bfloat16):
    array = spread * jax.random.normal(rng, shape, jnp.float32)
    if pieces:
        array = array * block_levels(rng, shape, pieces, -0.22, 0.18)
    return jnp.clip(with_spikes(array, jax.random.fold_in(rng, 3), *heavy), -reach, reach).astype(dtype)


def setup_inputs(seed: int = 0) -> dict:
    arg_keys = jax.random.split(jax.random.key(seed), 6)
    return {
        "tokens": heavy_noise(arg_keys[0], (TOKENS, D), 1.0, 24.0, ((0, 128),), (0, 1, 128, 5.5)),
        "cotangent": gaussian(arg_keys[1], (TOKENS, FF), 2.0, 12.0, ((0, 128),)),
        "master": gaussian(arg_keys[2], (FF, D), D ** -0.5, 0.046875, ((0, 8), (1, 16)), jnp.float32),
        "moment_one": gaussian(arg_keys[3], (FF, D), 1.0, 6.0, ((0, 8), (1, 16)), jnp.float32),
        "moment_two": jnp.clip(jnp.exp(math.log(8.0) - 2.7725887 * jax.random.uniform(arg_keys[4], (FF, D), jnp.float32) ** block_levels(arg_keys[4], (FF, D), ((0, 8), (1, 16)), -0.2, 0.2)), 0.5, 8.0),
    }


beta_one = 0.9
beta_two = 0.95
learn_rate = 0.001
adam_eps = 1e-08
gelu_coef = 0.7978845608
gelu_cube = 0.044715

def gelu_value(pre_act):
    tanh_val = jnp.tanh(gelu_coef * (pre_act + gelu_cube * pre_act * pre_act * pre_act))
    return 0.5 * pre_act * (1.0 + tanh_val)

def gelu_slope(pre_act):
    tanh_val = jnp.tanh(gelu_coef * (pre_act + gelu_cube * pre_act * pre_act * pre_act))
    inner = gelu_coef * (1.0 + 3.0 * gelu_cube * pre_act * pre_act)
    return 0.5 * (1.0 + tanh_val) + 0.5 * pre_act * (1.0 - tanh_val * tanh_val) * inner

def reference(tokens, cotangent, master, moment_one, moment_two):
    weight_bf = master.astype(jnp.bfloat16)
    token_blocks = tokens.reshape(DEVICES, TOK_DEV, D)
    grad_blocks = cotangent.reshape(DEVICES, TOK_DEV, FF)

    def per_block(running, inputs):
        block_tokens, block_cot = inputs
        pre_act = jnp.dot(block_tokens, weight_bf.T, preferred_element_type=jnp.float32)
        hidden = gelu_value(pre_act).astype(jnp.bfloat16)
        act_grad = (block_cot.astype(jnp.float32) * gelu_slope(pre_act)).astype(jnp.bfloat16)
        input_grad = jnp.dot(act_grad, weight_bf, preferred_element_type=jnp.float32).astype(jnp.bfloat16)
        term_rows = jnp.dot(act_grad.T, block_tokens, preferred_element_type=jnp.float32)
        term_rows = lax.optimization_barrier(term_rows.astype(jnp.bfloat16)).astype(jnp.float32)
        return (running + term_rows, (hidden, input_grad))
    summed, (hidden_all, input_all) = lax.scan(per_block, jnp.zeros((FF, D), jnp.float32), (token_blocks, grad_blocks))
    gradient = summed / DEVICES
    moment_one_new = beta_one * moment_one + (1.0 - beta_one) * gradient
    moment_two_new = beta_two * moment_two + (1.0 - beta_two) * gradient * gradient
    first_fix = 1.0 - beta_one ** STEP
    second_fix = 1.0 - beta_two ** STEP
    master_new = master - learn_rate * (moment_one_new / first_fix) / (jnp.sqrt(moment_two_new / second_fix) + adam_eps)
    return (hidden_all.reshape(TOKENS, FF), input_all.reshape(TOKENS, D), gradient, master_new, moment_one_new, moment_two_new)
```

```python
import functools

import jax
import jax.numpy as jnp
from jax import lax
from jax.experimental import pallas as pl
from jax.experimental.pallas import tpu as pltpu
from jax.sharding import PartitionSpec as P

MESH = pl.DeviceIdType.MESH
STEP = 10

beta_one = 0.9
beta_two = 0.95
learn_rate = 0.001
adam_eps = 1e-08
gelu_coef = 0.7978845608
gelu_cube = 0.044715

ORDERS = (("x", "y", "z"), ("y", "z", "x"), ("z", "x", "y"))
ROWS = 16
PARTS = 3


def wrap(value):
    return lax.rem(value + 4, 4)


def flip(value):
    return value + 1 - 2 * lax.rem(value, 2)


def device(at, core):
    node = at["z"] * 4 + (at["y"] // 2) * 2 + core
    local = lax.rem(at["y"], 2) * 4 + at["x"]
    return (node, local)


def kernel(
    master, tokens, cot, out_grad, out_hidden, out_input,
    weights, tok, terms, acc, pre_in, act_t, act, cot_t, stage, hop_a, hop_b, hop_c, row_a, row_b, row_c, last_in,
    tok_sem, tok_send, tok_recv, pre_send, pre_recv, act_send, act_recv, in_send, in_recv,
    ag_send, ag_recv, rs_send, rs_recv,
):
    node, local = lax.axis_index("node"), lax.axis_index("local")
    core = lax.rem(node, 2)
    me = {"x": lax.rem(local, 4), "y": lax.rem(node // 2, 2) * 2 + local // 4, "z": node // 4}
    sign = 1 - 2 * core
    width = master.shape[1]
    half = tokens.shape[0]

    def near(dim, step):
        at = dict(me)
        at[dim] = wrap(at[dim] + step)
        return device(at, core)

    partner = device(me, 1 - core)
    around = [near(dim, step) for dim in "xyz" for step in (1, 3, 2)] + [partner]
    barrier = pltpu.get_barrier_semaphore()
    for other in around:
        pl.semaphore_signal(barrier, inc=1, device_id=other, device_id_type=MESH)

    own_tok = [
        pltpu.make_async_copy(
            tokens.at[:, pl.ds(pl.multiple_of((2 * k + core) * width, 128), width)],
            tok.at[k, pl.ds(pl.multiple_of(core * half, half), half), :],
            tok_sem.at[k],
        )
        for k in range(8)
    ]
    for copy in own_tok:
        copy.start()
    weights[me["z"], me["y"], me["x"]] = master[...].astype(jnp.bfloat16)
    pl.semaphore_wait(barrier, len(around))

    sent = []

    def send(src, dst, send_sem, recv_sem, to):
        copy = pltpu.make_async_remote_copy(
            src_ref=src, dst_ref=dst, send_sem=send_sem, recv_sem=recv_sem, device_id=to, device_id_type=MESH
        )
        copy.start()
        sent.append(copy)

    def arrived(dst, send_sem, recv_sem):
        pltpu.make_async_remote_copy(
            src_ref=dst, dst_ref=dst, send_sem=send_sem, recv_sem=recv_sem, device_id=partner, device_id_type=MESH
        ).wait_recv()

    def block(buf, part, place):
        return buf.at[
            tuple(pl.ds(0, 4) if place[d] is None else place[d] for d in "zyx")
            + (pl.ds(part * ROWS, ROWS), slice(None))
        ]

    def ag(part, msg, src_place, to):
        region = block(weights, part, src_place)
        send(region, region, ag_send.at[part, msg], ag_recv.at[part, msg], to)

    def ag_wait(part, msg, place):
        arrived(block(weights, part, place), ag_send.at[part, msg], ag_recv.at[part, msg])

    for i, step in enumerate((1, 3, 2)):
        for part, (one, two, three) in enumerate(ORDERS):
            ag(part, i, me, near(one, step))
    for k in range(8):
        send(
            tokens.at[:, pl.ds(pl.multiple_of((2 * k + 1 - core) * width, 128), width)],
            tok.at[k, pl.ds(pl.multiple_of(core * half, half), half), :],
            tok_send.at[k],
            tok_recv.at[k],
            partner,
        )
    cot_t[...] = cot[...].astype(jnp.float32).T.astype(jnp.bfloat16)
    for i, step in enumerate((1, 3, 2)):
        for part, (one, two, three) in enumerate(ORDERS):
            ag_wait(part, i, {**me, one: wrap(me[one] - step)})

    def rows_of(dim):
        return (me[dim], wrap(me[dim] - sign), wrap(me[dim] + sign), wrap(me[dim] + 2))

    def row(part, which, plane):
        one, two, three = ORDERS[part]
        return {one: None, two: rows_of(two)[which], three: rows_of(three)[plane]}

    def second(part, which):
        two = ORDERS[part][1]
        if which == 2:
            ag(part, 5, row(part, 1, 0), near(two, sign))
        else:
            ag(part, 3 + which, row(part, 0, 0), near(two, sign if which == 0 else -sign))

    def third(part, which, kind):
        three = ORDERS[part][2]
        if kind == 2:
            ag(part, 6 + 3 * which + 2, row(part, which, 1), near(three, sign))
        else:
            ag(part, 6 + 3 * which + kind, row(part, which, 0), near(three, sign if kind == 0 else -sign))

    def third_wait(part, which, kind):
        ag_wait(part, 6 + 3 * which + kind, row(part, which, kind + 1))

    every = range(PARTS)
    for part in every:
        second(part, 0)
        second(part, 1)
    for part in every:
        third(part, 0, 0)
        third(part, 0, 1)
    for part in every:
        ag_wait(part, 3, row(part, 1, 0))
        second(part, 2)
        third(part, 1, 0)
        third(part, 1, 1)
    for part in every:
        ag_wait(part, 4, row(part, 2, 0))
        third(part, 2, 0)
        third(part, 2, 1)
    for part in every:
        third_wait(part, 0, 0)
        third(part, 0, 2)
    for part in every:
        ag_wait(part, 5, row(part, 3, 0))
        third(part, 3, 0)
        third(part, 3, 1)
    for which in (1, 2, 3):
        for part in every:
            third_wait(part, which, 0)
            third(part, which, 2)
    acc[...] = jnp.zeros_like(acc)
    for k in range(8):
        own_tok[k].wait()
        arrived(
            tok.at[k, pl.ds(pl.multiple_of((1 - core) * half, half), half), :], tok_send.at[k], tok_recv.at[k]
        )
    for which in range(4):
        for part in every:
            third_wait(part, which, 1)
    for which in range(4):
        for part in every:
            third_wait(part, which, 2)

    def chunk_of(buf, z, upper):
        units = 8 * PARTS * ROWS
        return buf[z, pl.ds(2 * upper, 2)].reshape(units, width)

    def forward(k, carry):
        acc[...] += lax.dot_general(
            chunk_of(weights, k // 2, lax.rem(k, 2)), tok[k], (((1,), (1,)), ((), ())),
            preferred_element_type=jnp.float32,
        )
        return carry

    lax.fori_loop(0, 8, forward, 0)

    mine = pl.ds(pl.multiple_of(core * half, half), half)
    theirs = pl.ds(pl.multiple_of((1 - core) * half, half), half)
    send(acc.at[:, theirs], pre_in, pre_send, pre_recv, partner)
    arrived(pre_in, pre_send, pre_recv)
    pre = acc[:, mine] + pre_in[...]
    tanh_val = jnp.tanh(gelu_coef * (pre + gelu_cube * pre * pre * pre))
    inner = gelu_coef * (1.0 + 3.0 * gelu_cube * pre * pre)
    slope = 0.5 * (1.0 + tanh_val) + 0.5 * pre * (1.0 - tanh_val * tanh_val) * inner
    act_t[:, mine] = (cot_t[...].astype(jnp.float32) * slope).astype(jnp.bfloat16)
    send(act_t.at[:, mine], act_t.at[:, mine], act_send, act_recv, partner)
    out_hidden[...] = (0.5 * pre * (1.0 + tanh_val)).T.astype(jnp.bfloat16)
    arrived(act_t.at[:, theirs], act_send, act_recv)

    def term(z, upper):
        value = jnp.dot(act_t[...], tok[2 * z + upper], preferred_element_type=jnp.float32)
        terms[z, pl.ds(2 * upper, 2)] = value.astype(jnp.bfloat16).reshape(2, 4, PARTS * ROWS, width)

    def order(dim):
        far = wrap(me[dim] + 2)
        return (far, flip(far), flip(me[dim]), me[dim])

    def term_row(part, which, plane):
        one, two, three = ORDERS[part]
        return block(terms, part, {one: None, two: order(two)[which], three: wrap(me[three] + plane)})

    def rs(part, msg, src, dst, to):
        send(src, dst, rs_send.at[part, msg], rs_recv.at[part, msg], to)

    def rs_wait(part, msg, dst):
        arrived(dst, rs_send.at[part, msg], rs_recv.at[part, msg])

    def far_send(part, which):
        rs(part, which, term_row(part, which, 2), hop_a.at[part, which], near(ORDERS[part][2], sign))

    def back_send(part, which):
        rs(part, 8 + which, term_row(part, which, -sign), hop_c.at[part, which], near(ORDERS[part][2], -sign))

    def sum_into(dst, *terms_in):
        total = terms_in[0][...].astype(jnp.float32)
        for value in terms_in[1:]:
            total += value[...].astype(jnp.float32)
        dst[...] = total.astype(dst.dtype)

    up = me["y"] // 2
    zs = (wrap(me["z"] + 2), wrap(me["z"] - sign), wrap(me["z"] + sign), me["z"])
    for upper_is_far in (1, 0):
        upper = 1 - up if upper_is_far else up
        for i, z in enumerate(zs):
            term(z, upper)
            if i == 0:
                for which in (0, 1) if upper_is_far else (2, 3):
                    far_send(0, which)
            if i == 1:
                for which in (0, 1) if upper_is_far else (2, 3):
                    back_send(0, which)
            if not upper_is_far:
                which = {0: 0, 3: 3}.get(i)
                if which is not None:
                    far_send(1, which)
                    back_send(1, which)
                if i == 2:
                    for which in (1, 2):
                        far_send(1, which)
                        back_send(1, which)
        if upper_is_far:
            for which in range(4):
                far_send(2, which)
    for which in range(4):
        back_send(2, which)

    act[...] = act_t[...].astype(jnp.float32).T.astype(jnp.bfloat16)

    def input_chunk(k):
        z, upper = k // 2, k % 2
        weight = chunk_of(weights, z, upper)
        columns = pl.ds(pl.multiple_of((2 * k + core) * width, 128), width)
        stage[k] = jnp.dot(act[theirs, :], weight, preferred_element_type=jnp.float32).astype(jnp.bfloat16)
        send(stage.at[k], out_input.at[:, columns], in_send.at[k], in_recv.at[k], partner)
        out_input[:, columns] = jnp.dot(act[mine, :], weight, preferred_element_type=jnp.float32).astype(
            jnp.bfloat16
        )

    for k in range(2):
        input_chunk(k)
    for which in range(4):
        for part in every:
            rs_wait(part, which, hop_a.at[part, which])
            sum_into(hop_a.at[part, which], hop_a.at[part, which], term_row(part, which, sign))
            rs(part, 4 + which, hop_a.at[part, which], hop_b.at[part, which], near(ORDERS[part][2], sign))
        input_chunk(2 + which)

    def second_row(part, plane):
        one, two, three = ORDERS[part]
        return block(terms, part, {one: None, two: wrap(me[two] + plane), three: me[three]})

    for which in range(4):
        for part in every:
            rs_wait(part, 4 + which, hop_b.at[part, which])
            rs_wait(part, 8 + which, hop_c.at[part, which])
            here = term_row(part, which, 0)
            sum_into(here, here, hop_b.at[part, which], hop_c.at[part, which])
        for part in every:
            two = ORDERS[part][1]
            if which == 0:
                rs(part, 12, second_row(part, 2), row_a.at[part], near(two, sign))
            if which == 2:
                rs(part, 14, second_row(part, -sign), row_c.at[part], near(two, -sign))
        if which == 2:
            for part in every:
                rs_wait(part, 12, row_a.at[part])
                sum_into(row_a.at[part], row_a.at[part], second_row(part, sign))
                rs(part, 13, row_a.at[part], row_b.at[part], near(ORDERS[part][1], sign))
            input_chunk(6)
            input_chunk(7)

    for part in every:
        rs_wait(part, 13, row_b.at[part])
        rs_wait(part, 14, row_c.at[part])
        here = second_row(part, 0)
        sum_into(here, here, row_b.at[part], row_c.at[part])
        one = ORDERS[part][0]
        for i, step in enumerate((2, 1, 3)):
            rs(
                part, 15 + i, block(terms, part, {**me, one: wrap(me[one] + step)}), last_in.at[part, i],
                near(one, step),
            )
    for part in every:
        for i in range(3):
            rs_wait(part, 15 + i, last_in.at[part, i])
        sum_into(
            out_grad.at[pl.ds(part * ROWS, ROWS), :], block(terms, part, me), *(last_in.at[part, i] for i in range(3))
        )

    for k in range(8):
        arrived(
            out_input.at[:, pl.ds(pl.multiple_of((2 * k + 1 - core) * width, 128), width)], in_send.at[k], in_recv.at[k]
        )
    for copy in sent:
        copy.wait_send()


def shards(tokens, cotangent, master, moment_one, moment_two):
    half, model = tokens.shape
    units, width = master.shape
    all_units = cotangent.shape[1]
    bf, f32 = jnp.bfloat16, jnp.float32
    dma = pltpu.SemaphoreType.DMA
    vmem = pl.BlockSpec(memory_space=pltpu.VMEM)
    total, hidden, input_grad = pl.pallas_call(
        kernel,
        out_shape=(
            jax.ShapeDtypeStruct((units, width), f32),
            jax.ShapeDtypeStruct((half, all_units), bf),
            jax.ShapeDtypeStruct((half, model), bf),
        ),
        in_specs=[vmem, pl.BlockSpec(memory_space=pl.ANY), vmem],
        out_specs=(vmem, vmem, vmem),
        scratch_shapes=[
            pltpu.VMEM((4, 4, 4, units, width), bf),
            pltpu.VMEM((8, 2 * half, width), bf),
            pltpu.VMEM((4, 4, 4, units, width), bf),
            pltpu.VMEM((all_units, 2 * half), f32),
            pltpu.VMEM((all_units, half), f32),
            pltpu.VMEM((all_units, 2 * half), bf),
            pltpu.VMEM((2 * half, all_units), bf),
            pltpu.VMEM((all_units, half), bf),
            pltpu.VMEM((8, half, width), bf),
            pltpu.VMEM((PARTS, 4, 4, ROWS, width), bf),
            pltpu.VMEM((PARTS, 4, 4, ROWS, width), bf),
            pltpu.VMEM((PARTS, 4, 4, ROWS, width), bf),
            pltpu.VMEM((PARTS, 4, ROWS, width), bf),
            pltpu.VMEM((PARTS, 4, ROWS, width), bf),
            pltpu.VMEM((PARTS, 4, ROWS, width), bf),
            pltpu.VMEM((PARTS, 3, ROWS, width), bf),
            dma((8,)), dma((8,)), dma((8,)), dma, dma, dma, dma, dma((8,)), dma((8,)),
            dma((PARTS, 18)), dma((PARTS, 18)), dma((PARTS, 18)), dma((PARTS, 18)),
        ],
        compiler_params=pltpu.CompilerParams(
            collective_id=0, has_side_effects=True, vmem_limit_bytes=56 * 2**20
        ),
        name="gather_project_scatter",
    )(master, tokens, cotangent)
    gradient = total / (lax.axis_size("node") * lax.axis_size("local"))
    moment_one_new = beta_one * moment_one + (1.0 - beta_one) * gradient
    moment_two_new = beta_two * moment_two + (1.0 - beta_two) * gradient * gradient
    first_fix = 1.0 - beta_one**STEP
    second_fix = 1.0 - beta_two**STEP
    master_new = master - learn_rate * (moment_one_new / first_fix) / (
        jnp.sqrt(moment_two_new / second_fix) + adam_eps
    )
    return (hidden, input_grad, gradient, master_new, moment_one_new, moment_two_new)


def solution(mesh):
    in_specs = (
        P(("node", "local"), None),
        P(("node", "local"), None),
        P("local", "node"),
        P("local", "node"),
        P("local", "node"),
    )
    out_specs = (
        P(("node", "local"), None),
        P(("node", "local"), None),
        P("local", "node"),
        P("local", "node"),
        P("local", "node"),
        P("local", "node"),
    )
    return jax.shard_map(shards, mesh=mesh, in_specs=in_specs, out_specs=out_specs, check_vma=False)
```

```python
import functools

import jax
import jax.numpy as jnp
from jax import lax
from jax.experimental import pallas as pl
from jax.experimental.pallas import tpu as pltpu
from jax.sharding import PartitionSpec as P

MESH = pl.DeviceIdType.MESH
STEP = 10

beta_one = 0.9
beta_two = 0.95
learn_rate = 0.001
adam_eps = 1e-08
gelu_coef = 0.7978845608
gelu_cube = 0.044715

ORDERS = (("x", "y", "z"), ("y", "z", "x"), ("z", "x", "y"))
ROWS = 16
GROUPS = 3
COLUMNS = ((0, 384), (384, 256), (640, 256))
WIDEST = 384
AG_DIRECT = (True, False, False)
RS_DIRECT = (False, False, True)


(
    LINE, PLANE, PLANE_ON, CUBE, CUBE_ON, TOKENS_OUT, TOKENS_IN, COT_TURN, FORWARD, PARTIAL_OUT,
    ACTIVATE, TERM, FAR, BACK, RS_CUBE_ON, RS_PLANE, RS_PLANE_ON, RS_LINE, RS_END, ACT_TURN, INPUT,
    HIDDEN,
) = range(22)
SCHEDULE = (
    (LINE, 0, 2), (LINE, 0, 0), (LINE, 0, 1), (LINE, 1, 0), (LINE, 2, 2), (TOKENS_OUT,), (LINE, 2, 0), (LINE, 2, 1),
    (LINE, 1, 1), (LINE, 1, 2), (PLANE, 0, 2), (PLANE, 0, 1), (PLANE, 0, 0), (PLANE, 1, 0), (PLANE, 1, 2),
    (PLANE, 1, 1), (PLANE, 2, 2), (PLANE, 2, 1), (CUBE, 0, 1, 0), (CUBE, 0, 2, 0), (CUBE, 0, 0, 0), (PLANE_ON, 1, 2),
    (CUBE, 0, 2, 1), (CUBE, 0, 1, 1), (CUBE, 0, 0, 1), (TOKENS_IN, 0), (FORWARD, 0, 0, 0), (PLANE, 2, 0),
    (PLANE_ON, 1, 1), (CUBE, 1, 1, 0), (CUBE_ON, 0, 1, 0), (PLANE_ON, 1, 0), (CUBE_ON, 0, 2, 0), (CUBE_ON, 0, 2, 1),
    (CUBE, 1, 2, 0), (CUBE, 1, 2, 1), (CUBE_ON, 0, 1, 1), (TOKENS_IN, 1), (CUBE_ON, 0, 0, 0), (TOKENS_IN, 2),
    (COT_TURN,), (CUBE_ON, 0, 0, 1), (CUBE, 1, 0, 0), (FORWARD, 0, 0, 1), (TOKENS_IN, 3), (CUBE, 1, 0, 1),
    (PLANE_ON, 2, 0), (CUBE_ON, 1, 1, 0), (FORWARD, 1, 0, 0), (FORWARD, 0, 2, 0), (PLANE_ON, 2, 2),
    (FORWARD, 0, 0, 2), (CUBE, 2, 2, 0), (CUBE, 1, 1, 1), (FORWARD, 0, 2, 1), (FORWARD, 0, 1, 0), (FORWARD, 0, 1, 1),
    (FORWARD, 0, 0, 3), (PARTIAL_OUT, 0), (PLANE_ON, 2, 1), (CUBE, 2, 1, 0), (CUBE, 2, 0, 0), (CUBE_ON, 1, 2, 0),
    (CUBE_ON, 1, 2, 1), (FORWARD, 1, 1, 0), (CUBE, 2, 2, 1), (FORWARD, 1, 2, 0), (CUBE_ON, 1, 1, 1),
    (CUBE_ON, 1, 0, 0), (CUBE_ON, 1, 0, 1), (FORWARD, 1, 0, 1), (CUBE, 2, 0, 1), (ACTIVATE, 0), (TERM, 0, 0),
    (FAR, 0, 0, 1), (CUBE, 2, 1, 1), (TERM, 0, 1), (TERM, 0, 2), (BACK, 0, 0, 0), (CUBE_ON, 2, 0, 0), (FAR, 0, 2, 1),
    (FAR, 0, 2, 0), (TERM, 0, 3), (BACK, 0, 2, 1), (FAR, 0, 1, 1), (FAR, 0, 1, 0), (FORWARD, 1, 0, 2),
    (FORWARD, 1, 2, 1), (FORWARD, 1, 1, 1), (BACK, 0, 1, 0), (FORWARD, 1, 0, 3), (PARTIAL_OUT, 1), (CUBE_ON, 2, 2, 0),
    (BACK, 0, 2, 0), (CUBE_ON, 2, 0, 1), (BACK, 0, 1, 1), (CUBE_ON, 2, 2, 1), (BACK, 0, 0, 1), (CUBE_ON, 2, 1, 0),
    (CUBE_ON, 2, 1, 1), (FORWARD, 2, 2, 0), (FORWARD, 2, 0, 1), (FORWARD, 2, 0, 0), (FORWARD, 2, 0, 2),
    (RS_CUBE_ON, 0, 1, 1), (RS_CUBE_ON, 0, 2, 1), (FAR, 0, 0, 0), (RS_CUBE_ON, 0, 0, 1), (RS_CUBE_ON, 0, 1, 0),
    (ACTIVATE, 1), (TERM, 1, 0), (TERM, 1, 1), (FAR, 1, 2, 1), (FAR, 1, 2, 0), (TERM, 1, 2), (TERM, 1, 3),
    (BACK, 1, 2, 0), (FAR, 1, 0, 1), (FAR, 1, 1, 1), (FAR, 1, 1, 0), (FORWARD, 2, 1, 0), (FORWARD, 2, 0, 3),
    (FORWARD, 2, 1, 1), (BACK, 1, 2, 1), (FORWARD, 2, 2, 1), (PARTIAL_OUT, 2), (FAR, 1, 0, 0), (BACK, 1, 0, 0),
    (BACK, 1, 0, 1), (BACK, 1, 1, 1), (BACK, 1, 1, 0), (RS_PLANE, 0, 2, 1), (RS_CUBE_ON, 0, 2, 0),
    (RS_PLANE, 0, 1, 1), (RS_CUBE_ON, 0, 0, 0), (RS_CUBE_ON, 1, 2, 1), (RS_CUBE_ON, 1, 2, 0), (RS_CUBE_ON, 1, 1, 1),
    (RS_PLANE, 0, 0, 1), (ACTIVATE, 2), (TERM, 2, 0), (TERM, 2, 1), (FAR, 2, 2, 1), (FAR, 2, 0, 1),
    (RS_CUBE_ON, 1, 0, 1), (RS_CUBE_ON, 1, 1, 0), (FAR, 2, 2, 0), (TERM, 2, 2), (FAR, 2, 0, 0), (TERM, 2, 3),
    (BACK, 2, 2, 0), (FAR, 2, 1, 1), (FAR, 2, 1, 0), (BACK, 2, 2, 1), (BACK, 2, 1, 0), (RS_CUBE_ON, 1, 0, 0),
    (ACT_TURN,), (INPUT, 0), (RS_PLANE, 1, 2, 1), (RS_PLANE, 1, 2, 0), (RS_PLANE, 1, 1, 1), (RS_CUBE_ON, 2, 0, 1),
    (BACK, 2, 0, 1), (BACK, 2, 0, 0), (BACK, 2, 1, 1), (RS_CUBE_ON, 2, 2, 1), (INPUT, 1), (RS_CUBE_ON, 2, 1, 1),
    (RS_CUBE_ON, 2, 2, 0), (RS_CUBE_ON, 2, 0, 0), (RS_PLANE, 0, 2, 0), (RS_PLANE, 1, 0, 1), (RS_CUBE_ON, 2, 1, 0),
    (RS_PLANE_ON, 0, 2), (RS_PLANE, 0, 0, 0), (RS_PLANE_ON, 0, 0), (RS_PLANE, 0, 1, 0), (RS_PLANE_ON, 1, 2),
    (RS_PLANE, 1, 1, 0), (RS_PLANE_ON, 1, 1), (INPUT, 2), (RS_PLANE, 2, 2, 1), (RS_PLANE, 2, 0, 1),
    (RS_PLANE, 2, 1, 1), (RS_PLANE, 1, 0, 0), (RS_PLANE, 2, 2, 0), (RS_PLANE_ON, 0, 1), (RS_PLANE_ON, 1, 0),
    (RS_PLANE, 2, 1, 0), (RS_PLANE, 2, 0, 0), (INPUT, 3), (RS_LINE, 0, 0), (RS_LINE, 1, 1), (RS_LINE, 0, 2),
    (RS_LINE, 1, 0), (RS_LINE, 1, 2), (RS_LINE, 0, 1), (RS_LINE, 2, 2), (RS_LINE, 2, 1), (RS_LINE, 2, 0),
    (RS_END, 1, 0), (RS_END, 0, 2), (HIDDEN,), (RS_END, 0, 1), (RS_END, 0, 0), (RS_END, 1, 2), (RS_END, 1, 1),
    (RS_END, 2, 1), (RS_END, 2, 2), (RS_END, 2, 0),
)


def wrap(value):
    return lax.rem(value + 4, 4)


def device(at, core):
    node = at["z"] * 4 + (at["y"] // 2) * 2 + core
    local = lax.rem(at["y"], 2) * 4 + at["x"]
    return (node, local)


def kernel(
    master_hbm, tokens, cot_hbm, out_grad, out_hidden, out_input,
    weights, tok, terms, acc, pre_in, act_t, act, cot_t, hid_t, stage, master, cot,
    hop_a0, hop_a1, hop_a2, hop_b0, hop_b1, hop_b2, hop_c0, hop_c1, hop_c2, row_a, row_b, row_c, last_in,
    own_sem, tok_sem, tok_send, tok_recv, pre_send, pre_recv, cot_send, cot_recv, in_send, in_recv,
    ag_send, ag_recv, rs_send, rs_recv,
):
    hop_a, hop_b, hop_c = (hop_a0, hop_a1, hop_a2), (hop_b0, hop_b1, hop_b2), (hop_c0, hop_c1, hop_c2)
    node, local = lax.axis_index("node"), lax.axis_index("local")
    core = lax.rem(node, 2)
    me = {"x": lax.rem(local, 4), "y": lax.rem(node // 2, 2) * 2 + local // 4, "z": node // 4}
    sign = 1 - 2 * core
    own = [
        pltpu.make_async_copy(master_hbm, master, own_sem.at[0]),
        pltpu.make_async_copy(cot_hbm, cot.at[core], own_sem.at[1]),
    ]
    for copy in own:
        copy.start()
    width = master.shape[1]
    half = tokens.shape[0]
    units = 8 * ROWS
    groups, orders = range(GROUPS), range(len(ORDERS))

    def near(dim, step):
        at = dict(me)
        at[dim] = wrap(at[dim] + step)
        return device(at, core)

    partner = device(me, 1 - core)
    around = [near(dim, step) for dim in "xyz" for step in (1, 3, 2)] + [partner]
    barrier = pltpu.get_barrier_semaphore()
    for other in around:
        pl.semaphore_signal(barrier, inc=1, device_id=other, device_id_type=MESH)

    mine = pl.ds(pl.multiple_of(core * half, half), half)
    theirs = pl.ds(pl.multiple_of((1 - core) * half, half), half)

    def columns_of(k, which):
        return pl.ds(pl.multiple_of((2 * k + which) * width, 128), width)

    def chunk(i):
        z = wrap(me["z"] + (0, -sign, sign, 2)[i // 2])
        return 2 * z + i % 2

    def own_tokens(i):
        k = chunk(i)
        return pltpu.make_async_copy(tokens.at[:, columns_of(k, core)], tok.at[k, mine, :], tok_sem.at[k])

    for i in range(8):
        own_tokens(i).start()
    own[0].wait()
    weights[me["z"], me["y"], me["x"]] = master[...].astype(jnp.bfloat16)
    acc[...] = jnp.zeros_like(acc)
    pl.semaphore_wait(barrier, len(around))

    sent = []

    def send(src, dst, send_sem, recv_sem, to):
        copy = pltpu.make_async_remote_copy(
            src_ref=src, dst_ref=dst, send_sem=send_sem, recv_sem=recv_sem, device_id=to, device_id_type=MESH
        )
        copy.start()
        sent.append(copy)

    def arrived(dst, send_sem, recv_sem):
        pltpu.make_async_remote_copy(
            src_ref=dst, dst_ref=dst, send_sem=send_sem, recv_sem=recv_sem, device_id=partner, device_id_type=MESH
        ).wait_recv()

    def columns(g, o):
        return COLUMNS[(o - g) % len(COLUMNS)]

    def block(buf, g, o, place):
        first, count = columns(g, o)
        return buf.at[tuple(place[d] for d in "zyx") + (pl.ds(g * ROWS, ROWS), pl.ds(first, count))]

    def cut(buf, g, o):
        return buf.at[..., pl.ds(0, columns(g, o)[1])]

    line = pl.ds(0, 4)

    def pair(dim, far):
        upper = me[dim] // 2
        return pl.ds(2 * (1 - upper if far else upper), 2)

    def ag(g, o, msg, place, to):
        region = block(weights, g, o, place)
        send(region, region, ag_send.at[3 * g + o, msg], ag_recv.at[3 * g + o, msg], to)

    def ag_wait(g, o, msg, place):
        arrived(block(weights, g, o, place), ag_send.at[3 * g + o, msg], ag_recv.at[3 * g + o, msg])

    def row(o, step):
        one, two, three = ORDERS[o]
        return {one: line, two: wrap(me[two] + step), three: me[three]}

    def rows(o, far, step):
        one, two, three = ORDERS[o]
        return {one: line, two: pair(two, far), three: wrap(me[three] + step)}

    def ag_line(g, o):
        for i, step in enumerate((1, 3, 2)):
            ag(g, o, i, me, near(ORDERS[o][0], step))

    def ag_plane(g, o):
        one, two, three = ORDERS[o]
        for i, step in enumerate((1, 3, 2)):
            ag_wait(g, o, i, {**me, one: wrap(me[one] - step)})
        ag(g, o, 3, row(o, 0), near(two, sign))
        ag(g, o, 4, row(o, 0), near(two, -sign))
        if AG_DIRECT[g]:
            ag(g, o, 5, row(o, 0), near(two, 2))

    def ag_plane_on(g, o):
        ag_wait(g, o, 3, row(o, -sign))
        ag(g, o, 5, row(o, -sign), near(ORDERS[o][1], sign))

    def ag_cube(g, o, far):
        three = ORDERS[o][2]
        if AG_DIRECT[g] and not far:
            ag_wait(g, o, 3, row(o, -sign))
        ag_wait(g, o, 4 + far, row(o, 2 if far else sign))
        ag(g, o, 6 + 3 * far, rows(o, far, 0), near(three, sign))
        ag(g, o, 7 + 3 * far, rows(o, far, 0), near(three, -sign))

    def ag_cube_on(g, o, far):
        ag_wait(g, o, 6 + 3 * far, rows(o, far, -sign))
        ag(g, o, 8 + 3 * far, rows(o, far, -sign), near(ORDERS[o][2], sign))

    def from_front(g, o, far):
        ag_wait(g, o, 7 + 3 * far, rows(o, far, sign))

    def from_across(g, o, far):
        ag_wait(g, o, 8 + 3 * far, rows(o, far, 2))

    def tokens_out():
        send(cot_hbm, cot.at[core], cot_send, cot_recv, partner)
        for i in range(8):
            k = chunk(i)
            send(tokens.at[:, columns_of(k, 1 - core)], tok.at[k, mine, :], tok_send.at[k], tok_recv.at[k], partner)

    def tokens_in(i):
        for j in (2 * i, 2 * i + 1):
            own_tokens(j).wait()
            k = chunk(j)
            arrived(tok.at[k, theirs, :], tok_send.at[k], tok_recv.at[k])

    def cot_turn():
        own[1].wait()
        arrived(cot.at[1 - core], cot_send, cot_recv)
        turned = cot[...].reshape(2 * half, GROUPS * units).astype(jnp.float32).T
        cot_t[...] = turned.astype(jnp.bfloat16).reshape(8, GROUPS, ROWS, 2 * half)

    def forward(g, o, i):
        if (o, i) in ((0, 2), (2, 0)):
            from_front(g, o, 0)
            from_front(g, o, 1)
        if (o, i) in ((0, 3), (2, 1)):
            from_across(g, o, 0)
            from_across(g, o, 1)
        if o == 1:
            from_front(g, o, i)
            from_across(g, o, i)
        first, count = columns(g, o)
        here = pl.ds(first, count)

        total = acc[g]
        for j in range(2 if o == 0 else 4):
            z, upper = j // 2, j % 2
            if o == 0:
                z = wrap(me["z"] + (0, -sign, sign, 2)[i])
            elif o == 1:
                z = lax.rem(me["z"] // 2 + i, 2) * 2 + z
            else:
                z, upper = j, lax.rem(me["y"] // 2 + i, 2)
            part = weights[z, pl.ds(2 * upper, 2), :, pl.ds(g * ROWS, ROWS), here].reshape(units, count)
            total += lax.dot_general(
                part, tok[2 * z + upper, :, here], (((1,), (1,)), ((), ())), preferred_element_type=jnp.float32
            )
        acc[g] = total

    def partial_out(g):
        send(acc.at[g], pre_in.at[g], pre_send.at[g], pre_recv.at[g], partner)

    def activate(g):
        arrived(pre_in.at[g], pre_send.at[g], pre_recv.at[g])
        pre = acc[g] + pre_in[g]
        tanh_val = jnp.tanh(gelu_coef * (pre + gelu_cube * pre * pre * pre))
        inner = gelu_coef * (1.0 + 3.0 * gelu_cube * pre * pre)
        slope = 0.5 * (1.0 + tanh_val) + 0.5 * pre * (1.0 - tanh_val * tanh_val) * inner
        slope *= cot_t[:, g].reshape(units, 2 * half).astype(jnp.float32)
        act_t[:, g] = slope.astype(jnp.bfloat16).reshape(8, ROWS, 2 * half)
        hid_t[:, g] = (0.5 * pre * (1.0 + tanh_val)).reshape(8, ROWS, 2 * half)

    def rs(g, o, msg, src, dst, to):
        send(src, dst, rs_send.at[3 * g + o, msg], rs_recv.at[3 * g + o, msg], to)

    def rs_wait(g, o, msg, dst):
        arrived(dst, rs_send.at[3 * g + o, msg], rs_recv.at[3 * g + o, msg])

    def add(dst, *values):
        total = values[0][...].astype(jnp.float32)
        for value in values[1:]:
            total += value[...].astype(jnp.float32)
        dst[...] = total.astype(dst.dtype)

    def term(g, i):
        upper = lax.rem(me["y"] // 2 + (1 if i < 2 else 0), 2)

        for step in (2, -sign) if i % 2 == 0 else (sign, 0):
            z = wrap(me["z"] + step)
            value = jnp.dot(act_t[:, g].reshape(units, 2 * half), tok[2 * z + upper], preferred_element_type=jnp.float32)
            terms[z, pl.ds(2 * upper, 2), :, pl.ds(g * ROWS, ROWS), :] = value.astype(jnp.bfloat16).reshape(
                2, 4, ROWS, width
            )

    def rs_far(g, o, far):
        hop = cut(hop_a[o].at[g, far], g, o)
        rs(g, o, 3 * far, block(terms, g, o, rows(o, far, 2)), hop, near(ORDERS[o][2], sign))

    def rs_back(g, o, far):
        hop = cut(hop_c[o].at[g, far], g, o)
        rs(g, o, 3 * far + 2, block(terms, g, o, rows(o, far, -sign)), hop, near(ORDERS[o][2], -sign))

    def add_pair(g, o, far, into_hop, plane, *hops):
        one, two, three = ORDERS[o]
        upper = me[two] // 2
        first = 2 * (1 - upper if far else upper)

        def step(i, carry):
            here = block(terms, g, o, {one: line, two: first + i, three: wrap(me[three] + plane)})
            views = [cut(hop.at[g, far, :, i] if o == 2 else hop.at[g, far, i], g, o) for hop in hops]
            add(views[0] if into_hop else here, here, *views)
            return carry

        lax.fori_loop(0, 2, step, 0)

    def rs_cube_on(g, o, far):
        hop = cut(hop_a[o].at[g, far], g, o)
        rs_wait(g, o, 3 * far, hop)
        add_pair(g, o, far, True, sign, hop_a[o])
        rs(g, o, 3 * far + 1, hop, cut(hop_b[o].at[g, far], g, o), near(ORDERS[o][2], sign))

    def rs_plane(g, o, far):
        rs_wait(g, o, 3 * far + 1, cut(hop_b[o].at[g, far], g, o))
        rs_wait(g, o, 3 * far + 2, cut(hop_c[o].at[g, far], g, o))
        add_pair(g, o, far, False, 0, hop_b[o], hop_c[o])
        two = ORDERS[o][1]
        if far:
            rs(g, o, 6, block(terms, g, o, row(o, 2)), cut(row_a.at[g, o], g, o), near(two, 2 if RS_DIRECT[g] else sign))
        else:
            rs(g, o, 8, block(terms, g, o, row(o, -sign)), cut(row_c.at[g, o], g, o), near(two, -sign))
            if RS_DIRECT[g]:
                rs(g, o, 7, block(terms, g, o, row(o, sign)), cut(row_b.at[g, o], g, o), near(two, sign))

    def rs_plane_on(g, o):
        here = cut(row_a.at[g, o], g, o)
        rs_wait(g, o, 6, here)
        add(here, here, block(terms, g, o, row(o, sign)))
        rs(g, o, 7, here, cut(row_b.at[g, o], g, o), near(ORDERS[o][1], sign))

    def rs_line(g, o):
        from_back, from_ahead = cut(row_b.at[g, o], g, o), cut(row_c.at[g, o], g, o)
        rs_wait(g, o, 7, from_back)
        rs_wait(g, o, 8, from_ahead)
        here = block(terms, g, o, row(o, 0))
        if RS_DIRECT[g]:
            across = cut(row_a.at[g, o], g, o)
            rs_wait(g, o, 6, across)
            add(here, here, from_back, from_ahead, across)
        else:
            add(here, here, from_back, from_ahead)
        one = ORDERS[o][0]
        for i, step in enumerate((2, 1, 3)):
            rs(
                g, o, 9 + i, block(terms, g, o, {**me, one: wrap(me[one] + step)}),
                cut(last_in.at[g, o, i], g, o), near(one, step),
            )

    def rs_end(g, o):
        views = [cut(last_in.at[g, o, i], g, o) for i in range(3)]
        for i, view in enumerate(views):
            rs_wait(g, o, 9 + i, view)
        first, count = columns(g, o)
        add(out_grad.at[pl.ds(g * ROWS, ROWS), pl.ds(first, count)], block(terms, g, o, me), *views)

    def act_turn():
        act[...] = act_t[...].reshape(GROUPS * units, 2 * half).astype(jnp.float32).T.astype(jnp.bfloat16)

    def hidden_turn():
        out_hidden[...] = hid_t[:, :, :, mine].reshape(GROUPS * units, half).T.astype(jnp.bfloat16)

    def input_chunks(i):
        for k in (2 * i, 2 * i + 1):
            weight = weights[k // 2, pl.ds(2 * (k % 2), 2)].reshape(GROUPS * units, width)
            here = columns_of(k, core)
            stage[k] = jnp.dot(act[theirs, :], weight, preferred_element_type=jnp.float32).astype(jnp.bfloat16)
            send(stage.at[k], out_input.at[:, here], in_send.at[k], in_recv.at[k], partner)
            out_input[:, here] = jnp.dot(act[mine, :], weight, preferred_element_type=jnp.float32).astype(jnp.bfloat16)

    steps = (
        ag_line, ag_plane, ag_plane_on, ag_cube, ag_cube_on, tokens_out, tokens_in, cot_turn, forward, partial_out,
        activate, term, rs_far, rs_back, rs_cube_on, rs_plane, rs_plane_on, rs_line, rs_end, act_turn, input_chunks,
        hidden_turn,
    )
    for name, *where in SCHEDULE:
        steps[name](*where)
    for k in range(8):
        arrived(out_input.at[:, columns_of(k, 1 - core)], in_send.at[k], in_recv.at[k])
    for copy in sent:
        copy.wait_send()


def update(
    blocks, total, hidden, input_grad, master, moment_one, moment_two,
    out_hidden, out_input, out_grad, out_master, out_one, out_two, old, new, in_sem, out_sem,
):
    loads = [
        pltpu.make_async_copy(value, old.at[i], in_sem.at[i]) for i, value in enumerate((moment_one, moment_two, master))
    ]
    for copy in loads:
        copy.start()
    rows = input_grad.shape[0] // 4
    copies = [
        pltpu.make_async_copy(
            input_grad.at[pl.ds(i * rows, rows)], out_input.at[pl.ds(i * rows, rows)], out_sem.at[i]
        )
        for i in range(4)
    ]
    copies.append(pltpu.make_async_copy(hidden, out_hidden, out_sem.at[4]))
    for copy in copies:
        copy.start()

    def store(i, value, out):
        new[i] = value
        copies.append(pltpu.make_async_copy(new.at[i], out, out_sem.at[5 + i]))
        copies[-1].start()

    gradient = total[...] / blocks
    store(0, gradient, out_grad)
    loads[0].wait()
    moment_one_new = beta_one * old[0] + (1.0 - beta_one) * gradient
    store(1, moment_one_new, out_one)
    loads[1].wait()
    moment_two_new = beta_two * old[1] + (1.0 - beta_two) * gradient * gradient
    store(2, moment_two_new, out_two)
    loads[2].wait()
    first_fix = 1.0 - beta_one**STEP
    second_fix = 1.0 - beta_two**STEP
    step = learn_rate * (moment_one_new / first_fix) / (jnp.sqrt(moment_two_new / second_fix) + adam_eps)
    store(3, old[2] - step, out_master)
    for copy in copies:
        copy.wait()


def shards(tokens, cotangent, master, moment_one, moment_two):
    half, model = tokens.shape
    units, width = master.shape
    all_units = cotangent.shape[1]
    bf, f32 = jnp.bfloat16, jnp.float32
    dma = pltpu.SemaphoreType.DMA
    vmem, anywhere = pl.BlockSpec(memory_space=pltpu.VMEM), pl.BlockSpec(memory_space=pl.ANY)
    total, hidden, input_grad = pl.pallas_call(
        kernel,
        out_shape=(
            pltpu.VMEM((units, width), f32),
            pltpu.VMEM((half, all_units), bf),
            pltpu.VMEM((half, model), bf),
        ),
        in_specs=[anywhere] * 3,
        out_specs=(vmem, vmem, vmem),
        scratch_shapes=[
            pltpu.VMEM((4, 4, 4, units, width), bf),
            pltpu.VMEM((8, 2 * half, width), bf),
            pltpu.VMEM((4, 4, 4, units, width), bf),
            pltpu.VMEM((GROUPS, 8 * ROWS, 2 * half), f32),
            pltpu.VMEM((GROUPS, 8 * ROWS, 2 * half), f32),
            pltpu.VMEM((8, GROUPS, ROWS, 2 * half), bf),
            pltpu.VMEM((2 * half, all_units), bf),
            pltpu.VMEM((8, GROUPS, ROWS, 2 * half), bf),
            pltpu.VMEM((8, GROUPS, ROWS, 2 * half), f32),
            pltpu.VMEM((8, half, width), bf),
            pltpu.VMEM((units, width), f32),
            pltpu.VMEM((2, half, all_units), bf),
            *(pltpu.VMEM((GROUPS, 2) + ((4, 2) if o == 2 else (2, 4)) + (ROWS, WIDEST), bf) for _ in "abc" for o in range(3)),
            pltpu.VMEM((GROUPS, 3, 4, ROWS, WIDEST), bf),
            pltpu.VMEM((GROUPS, 3, 4, ROWS, WIDEST), bf),
            pltpu.VMEM((GROUPS, 3, 4, ROWS, WIDEST), bf),
            pltpu.VMEM((GROUPS, 3, 3, ROWS, WIDEST), bf),
            dma((2,)), dma((8,)), dma((8,)), dma((8,)), dma((GROUPS,)), dma((GROUPS,)), dma, dma,
            dma((8,)), dma((8,)),
            dma((3 * GROUPS, 12)), dma((3 * GROUPS, 12)), dma((3 * GROUPS, 12)), dma((3 * GROUPS, 12)),
        ],
        compiler_params=pltpu.CompilerParams(
            collective_id=0, has_side_effects=True, vmem_limit_bytes=40 * 2**20
        ),
        name="gather_project_scatter",
    )(*(pltpu.with_memory_space_constraint(value, pltpu.HBM) for value in (master, tokens, cotangent)))
    state = jax.ShapeDtypeStruct((units, width), f32)
    in_vmem = (pltpu.with_memory_space_constraint(value, pltpu.VMEM) for value in (total, hidden, input_grad))
    return pl.pallas_call(
        functools.partial(update, lax.axis_size("node") * lax.axis_size("local")),
        out_shape=(
            jax.ShapeDtypeStruct((half, all_units), bf),
            jax.ShapeDtypeStruct((half, model), bf),
            state, state, state, state,
        ),
        in_specs=[vmem] * 3 + [anywhere] * 3,
        out_specs=(anywhere,) * 6,
        scratch_shapes=[pltpu.VMEM((3, units, width), f32), pltpu.VMEM((4, units, width), f32), dma((3,)), dma((9,))],
        compiler_params=pltpu.CompilerParams(vmem_limit_bytes=16 * 2**20),
        name="adam_and_store",
    )(*in_vmem, *(pltpu.with_memory_space_constraint(value, pltpu.HBM) for value in (master, moment_one, moment_two)))


def solution(mesh):
    in_specs = (
        P(("node", "local"), None),
        P(("node", "local"), None),
        P("local", "node"),
        P("local", "node"),
        P("local", "node"),
    )
    out_specs = (
        P(("node", "local"), None),
        P(("node", "local"), None),
        P("local", "node"),
        P("local", "node"),
        P("local", "node"),
        P("local", "node"),
    )
    return jax.shard_map(shards, mesh=mesh, in_specs=in_specs, out_specs=out_specs, check_vma=False)
```

```python
import functools

import jax
import jax.numpy as jnp
from jax import lax
from jax.experimental import pallas as pl
from jax.experimental.pallas import tpu as pltpu
from jax.sharding import PartitionSpec as P

MESH = pl.DeviceIdType.MESH
STEP = 10

beta_one = 0.9
beta_two = 0.95
learn_rate = 0.001
adam_eps = 1e-08
gelu_coef = 0.7978845608
gelu_cube = 0.044715

ORDERS = (("x", "y", "z"), ("y", "z", "x"), ("z", "x", "y"))
ROWS = 16
GROUPS = 3
COLUMNS = ((0, 384), (384, 256), (640, 256))
WIDEST = 384
AG_DIRECT = (True, False, False)
RS_DIRECT = (False, False, True)


(
    LINE, PLANE, PLANE_ON, CUBE, CUBE_ON, TOKENS_OUT, TOKENS_IN, COT_TURN, FORWARD, PARTIAL_OUT,
    ACTIVATE, TERM, FAR, BACK, RS_CUBE_ON, RS_PLANE, RS_PLANE_ON, RS_LINE, RS_END, ACT_TURN, INPUT,
    HIDDEN,
) = range(22)
SCHEDULE = (
    (LINE, 0, 2), (LINE, 0, 0), (LINE, 0, 1), (LINE, 1, 1), (LINE, 2, 2), (LINE, 2, 1), (TOKENS_OUT,), (LINE, 2, 0),
    (LINE, 1, 2), (LINE, 1, 0), (COT_TURN,), (PLANE, 0, 2), (PLANE, 0, 1), (PLANE, 0, 0), (PLANE, 2, 1),
    (PLANE, 1, 1), (PLANE, 1, 2), (PLANE, 1, 0), (PLANE, 2, 2), (CUBE, 0, 2, 0), (CUBE, 0, 1, 0), (CUBE, 0, 0, 0),
    (PLANE_ON, 1, 2), (CUBE, 0, 2, 1), (TOKENS_IN, 0), (TOKENS_IN, 1), (CUBE, 0, 1, 1), (PLANE, 2, 0),
    (CUBE, 0, 0, 1), (PLANE_ON, 1, 1), (CUBE, 1, 1, 0), (PLANE_ON, 1, 0), (CUBE_ON, 0, 2, 0), (FORWARD, 0, 0, 0),
    (CUBE_ON, 0, 2, 1), (CUBE_ON, 0, 1, 0), (CUBE, 1, 2, 0), (CUBE, 1, 2, 1), (TOKENS_IN, 2), (CUBE_ON, 0, 0, 0),
    (CUBE_ON, 0, 1, 1), (CUBE_ON, 0, 0, 1), (FORWARD, 0, 0, 1), (CUBE, 1, 0, 0), (CUBE, 1, 0, 1), (TOKENS_IN, 3),
    (PLANE_ON, 2, 0), (CUBE_ON, 1, 1, 0), (FORWARD, 0, 2, 0), (FORWARD, 0, 0, 2), (PLANE_ON, 2, 2), (CUBE, 2, 2, 0),
    (FORWARD, 1, 0, 0), (CUBE, 1, 1, 1), (FORWARD, 0, 2, 1), (FORWARD, 0, 1, 0), (FORWARD, 0, 1, 1),
    (FORWARD, 0, 0, 3), (PARTIAL_OUT, 0), (PLANE_ON, 2, 1), (CUBE, 2, 1, 0), (CUBE, 2, 0, 0), (CUBE_ON, 1, 2, 0),
    (CUBE_ON, 1, 2, 1), (CUBE_ON, 1, 0, 0), (FORWARD, 1, 1, 0), (CUBE, 2, 2, 1), (FORWARD, 1, 2, 0),
    (CUBE_ON, 1, 1, 1), (CUBE_ON, 1, 0, 1), (FORWARD, 1, 0, 1), (CUBE, 2, 0, 1), (ACTIVATE, 0), (TERM, 0, 0),
    (CUBE, 2, 1, 1), (TERM, 0, 1), (FAR, 0, 2, 1), (FAR, 0, 2, 0), (TERM, 0, 2), (TERM, 0, 3), (FAR, 0, 0, 1),
    (FAR, 0, 0, 0), (FAR, 0, 1, 1), (FAR, 0, 1, 0), (BACK, 0, 2, 0), (BACK, 0, 2, 1), (BACK, 0, 1, 0),
    (FORWARD, 1, 0, 2), (FORWARD, 1, 2, 1), (FORWARD, 1, 1, 1), (FORWARD, 1, 0, 3), (PARTIAL_OUT, 1),
    (CUBE_ON, 2, 1, 0), (CUBE_ON, 2, 1, 1), (CUBE_ON, 2, 0, 0), (CUBE_ON, 2, 0, 1), (BACK, 0, 1, 1), (BACK, 0, 0, 0),
    (CUBE_ON, 2, 2, 0), (CUBE_ON, 2, 2, 1), (FORWARD, 2, 2, 0), (FORWARD, 2, 0, 0), (FORWARD, 2, 0, 2),
    (BACK, 0, 0, 1), (RS_CUBE_ON, 0, 2, 1), (RS_CUBE_ON, 0, 1, 1), (FORWARD, 2, 0, 1), (RS_CUBE_ON, 0, 0, 1),
    (RS_CUBE_ON, 0, 1, 0), (ACTIVATE, 1), (TERM, 1, 0), (TERM, 1, 1), (TERM, 1, 2), (FAR, 1, 0, 1), (FAR, 1, 2, 1),
    (TERM, 1, 3), (FAR, 1, 2, 0), (BACK, 1, 2, 1), (BACK, 1, 2, 0), (FAR, 1, 1, 1), (FORWARD, 2, 1, 0),
    (FORWARD, 2, 1, 1), (FAR, 1, 1, 0), (FORWARD, 2, 0, 3), (FORWARD, 2, 2, 1), (PARTIAL_OUT, 2), (BACK, 1, 1, 1),
    (FAR, 1, 0, 0), (BACK, 1, 1, 0), (BACK, 1, 0, 0), (RS_CUBE_ON, 0, 2, 0), (RS_PLANE, 0, 1, 1),
    (RS_CUBE_ON, 1, 2, 1), (RS_CUBE_ON, 1, 2, 0), (RS_CUBE_ON, 1, 1, 1), (RS_CUBE_ON, 0, 0, 0), (RS_PLANE, 0, 0, 1),
    (RS_PLANE, 0, 2, 1), (BACK, 1, 0, 1), (ACTIVATE, 2), (TERM, 2, 0), (TERM, 2, 1), (ACT_TURN, 1), (INPUT, 0, 1),
    (FAR, 2, 2, 1), (RS_CUBE_ON, 1, 1, 0), (FAR, 2, 0, 1), (RS_CUBE_ON, 1, 0, 1), (RS_CUBE_ON, 1, 0, 0), (TERM, 2, 2),
    (FAR, 2, 0, 0), (FAR, 2, 2, 0), (BACK, 2, 0, 0), (TERM, 2, 3), (INPUT, 1, 1), (BACK, 2, 2, 0), (FAR, 2, 1, 1),
    (FAR, 2, 1, 0), (BACK, 2, 2, 1), (RS_PLANE, 1, 2, 1), (BACK, 2, 1, 1), (ACT_TURN, 0), (INPUT, 0, 0),
    (RS_CUBE_ON, 2, 0, 1), (BACK, 2, 0, 1), (BACK, 2, 1, 0), (RS_CUBE_ON, 2, 2, 1), (INPUT, 1, 0),
    (RS_CUBE_ON, 2, 1, 1), (RS_CUBE_ON, 2, 2, 0), (RS_PLANE, 1, 1, 1), (RS_PLANE, 1, 0, 1), (RS_CUBE_ON, 2, 1, 0),
    (RS_PLANE, 0, 2, 0), (RS_PLANE, 0, 0, 0), (RS_PLANE_ON, 0, 0), (RS_CUBE_ON, 2, 0, 0), (RS_PLANE, 0, 1, 0),
    (RS_PLANE_ON, 0, 1), (RS_PLANE_ON, 0, 2), (RS_PLANE, 1, 2, 0), (RS_PLANE_ON, 1, 2), (RS_PLANE, 1, 1, 0),
    (INPUT, 2, 0), (RS_PLANE, 2, 2, 1), (INPUT, 2, 1), (RS_PLANE, 1, 0, 0), (RS_PLANE, 2, 0, 1), (RS_PLANE, 2, 1, 1),
    (RS_PLANE, 2, 2, 0), (RS_PLANE_ON, 1, 1), (RS_PLANE_ON, 1, 0), (RS_PLANE, 2, 0, 0), (RS_PLANE, 2, 1, 0),
    (INPUT, 3, 1), (RS_LINE, 0, 1), (RS_LINE, 0, 2), (RS_LINE, 0, 0), (RS_LINE, 1, 2), (INPUT, 3, 0), (RS_LINE, 1, 1),
    (RS_LINE, 1, 0), (RS_LINE, 2, 2), (RS_LINE, 2, 1), (RS_LINE, 2, 0), (HIDDEN,), (RS_END, 0, 0), (RS_END, 1, 1),
    (RS_END, 0, 2), (RS_END, 0, 1), (RS_END, 1, 2), (RS_END, 2, 1), (RS_END, 2, 2), (RS_END, 1, 0), (RS_END, 2, 0),
)


def wrap(value):
    return lax.rem(value + 4, 4)


def device(at, core):
    node = at["z"] * 4 + (at["y"] // 2) * 2 + core
    local = lax.rem(at["y"], 2) * 4 + at["x"]
    return (node, local)


def kernel(
    master_hbm, tokens, cot_hbm, out_grad, out_hidden, out_input,
    weights, tok, terms, acc, pre_in, act_t, act, cot_t, hid_t, stage, master, cot,
    hop_a0, hop_a1, hop_a2, hop_b0, hop_b1, hop_b2, hop_c0, hop_c1, hop_c2, row_a, row_b, row_c, last_in,
    own_sem, tok_sem, tok_send, tok_recv, pre_send, pre_recv, cot_send, cot_recv, in_send, in_recv,
    ag_send, ag_recv, rs_send, rs_recv,
):
    hop_a, hop_b, hop_c = (hop_a0, hop_a1, hop_a2), (hop_b0, hop_b1, hop_b2), (hop_c0, hop_c1, hop_c2)
    node, local = lax.axis_index("node"), lax.axis_index("local")
    core = lax.rem(node, 2)
    me = {"x": lax.rem(local, 4), "y": lax.rem(node // 2, 2) * 2 + local // 4, "z": node // 4}
    sign = 1 - 2 * core
    own = [
        pltpu.make_async_copy(master_hbm, master, own_sem.at[0]),
        pltpu.make_async_copy(cot_hbm, cot.at[core], own_sem.at[1]),
    ]
    for copy in own:
        copy.start()
    width = master.shape[1]
    half = tokens.shape[0]
    units = 8 * ROWS
    groups, orders = range(GROUPS), range(len(ORDERS))

    def near(dim, step):
        at = dict(me)
        at[dim] = wrap(at[dim] + step)
        return device(at, core)

    partner = device(me, 1 - core)
    around = [near(dim, step) for dim in "xyz" for step in (1, 3, 2)] + [partner]
    barrier = pltpu.get_barrier_semaphore()
    for other in around:
        pl.semaphore_signal(barrier, inc=1, device_id=other, device_id_type=MESH)

    mine = pl.ds(pl.multiple_of(core * half, half), half)
    theirs = pl.ds(pl.multiple_of((1 - core) * half, half), half)

    def columns_of(k, which):
        return pl.ds(pl.multiple_of((2 * k + which) * width, 128), width)

    def chunk(i):
        z = wrap(me["z"] + (0, -sign, sign, 2)[i // 2])
        return 2 * z + i % 2

    def own_tokens(i):
        k = chunk(i)
        return pltpu.make_async_copy(tokens.at[:, columns_of(k, core)], tok.at[k, mine, :], tok_sem.at[k])

    for i in range(8):
        own_tokens(i).start()
    own[0].wait()
    weights[me["z"], me["y"], me["x"]] = master[...].astype(jnp.bfloat16)
    acc[...] = jnp.zeros_like(acc)
    pl.semaphore_wait(barrier, len(around))

    sent = []

    def send(src, dst, send_sem, recv_sem, to):
        copy = pltpu.make_async_remote_copy(
            src_ref=src, dst_ref=dst, send_sem=send_sem, recv_sem=recv_sem, device_id=to, device_id_type=MESH
        )
        copy.start()
        sent.append(copy)

    def arrived(dst, send_sem, recv_sem):
        pltpu.make_async_remote_copy(
            src_ref=dst, dst_ref=dst, send_sem=send_sem, recv_sem=recv_sem, device_id=partner, device_id_type=MESH
        ).wait_recv()

    def columns(g, o):
        return COLUMNS[(o - g) % len(COLUMNS)]

    def block(buf, g, o, place):
        first, count = columns(g, o)
        return buf.at[tuple(place[d] for d in "zyx") + (pl.ds(g * ROWS, ROWS), pl.ds(first, count))]

    def cut(buf, g, o):
        return buf.at[..., pl.ds(0, columns(g, o)[1])]

    line = pl.ds(0, 4)

    def pair(dim, far):
        upper = me[dim] // 2
        return pl.ds(2 * (1 - upper if far else upper), 2)

    def ag(g, o, msg, place, to):
        region = block(weights, g, o, place)
        send(region, region, ag_send.at[3 * g + o, msg], ag_recv.at[3 * g + o, msg], to)

    def ag_wait(g, o, msg, place):
        arrived(block(weights, g, o, place), ag_send.at[3 * g + o, msg], ag_recv.at[3 * g + o, msg])

    def row(o, step):
        one, two, three = ORDERS[o]
        return {one: line, two: wrap(me[two] + step), three: me[three]}

    def rows(o, far, step):
        one, two, three = ORDERS[o]
        return {one: line, two: pair(two, far), three: wrap(me[three] + step)}

    def ag_line(g, o):
        for i, step in enumerate((1, 3, 2)):
            ag(g, o, i, me, near(ORDERS[o][0], step))

    def ag_plane(g, o):
        one, two, three = ORDERS[o]
        for i, step in enumerate((1, 3, 2)):
            ag_wait(g, o, i, {**me, one: wrap(me[one] - step)})
        ag(g, o, 3, row(o, 0), near(two, sign))
        ag(g, o, 4, row(o, 0), near(two, -sign))
        if AG_DIRECT[g]:
            ag(g, o, 5, row(o, 0), near(two, 2))

    def ag_plane_on(g, o):
        ag_wait(g, o, 3, row(o, -sign))
        ag(g, o, 5, row(o, -sign), near(ORDERS[o][1], sign))

    def ag_cube(g, o, far):
        three = ORDERS[o][2]
        if AG_DIRECT[g] and not far:
            ag_wait(g, o, 3, row(o, -sign))
        ag_wait(g, o, 4 + far, row(o, 2 if far else sign))
        ag(g, o, 6 + 3 * far, rows(o, far, 0), near(three, sign))
        ag(g, o, 7 + 3 * far, rows(o, far, 0), near(three, -sign))

    def ag_cube_on(g, o, far):
        ag_wait(g, o, 6 + 3 * far, rows(o, far, -sign))
        ag(g, o, 8 + 3 * far, rows(o, far, -sign), near(ORDERS[o][2], sign))

    def from_front(g, o, far):
        ag_wait(g, o, 7 + 3 * far, rows(o, far, sign))

    def from_across(g, o, far):
        ag_wait(g, o, 8 + 3 * far, rows(o, far, 2))

    def tokens_out():
        send(cot_hbm, cot.at[core], cot_send, cot_recv, partner)
        for i in range(8):
            k = chunk(i)
            send(tokens.at[:, columns_of(k, 1 - core)], tok.at[k, mine, :], tok_send.at[k], tok_recv.at[k], partner)

    def tokens_in(i):
        for j in (2 * i, 2 * i + 1):
            own_tokens(j).wait()
            k = chunk(j)
            arrived(tok.at[k, theirs, :], tok_send.at[k], tok_recv.at[k])

    def cot_turn():
        own[1].wait()
        arrived(cot.at[1 - core], cot_send, cot_recv)
        turned = cot[...].reshape(2 * half, GROUPS * units).astype(jnp.float32).T
        cot_t[...] = turned.astype(jnp.bfloat16).reshape(8, GROUPS, ROWS, 2 * half)

    def forward(g, o, i):
        if (o, i) in ((0, 2), (2, 0)):
            from_front(g, o, 0)
            from_front(g, o, 1)
        if (o, i) in ((0, 3), (2, 1)):
            from_across(g, o, 0)
            from_across(g, o, 1)
        if o == 1:
            from_front(g, o, i)
            from_across(g, o, i)
        first, count = columns(g, o)
        here = pl.ds(first, count)

        total = acc[g]
        for j in range(2 if o == 0 else 4):
            z, upper = j // 2, j % 2
            if o == 0:
                z = wrap(me["z"] + (0, -sign, sign, 2)[i])
            elif o == 1:
                z = lax.rem(me["z"] // 2 + i, 2) * 2 + z
            else:
                z, upper = j, lax.rem(me["y"] // 2 + i, 2)
            part = weights[z, pl.ds(2 * upper, 2), :, pl.ds(g * ROWS, ROWS), here].reshape(units, count)
            total += lax.dot_general(
                part, tok[2 * z + upper, :, here], (((1,), (1,)), ((), ())), preferred_element_type=jnp.float32
            )
        acc[g] = total

    def partial_out(g):
        send(acc.at[g], pre_in.at[g], pre_send.at[g], pre_recv.at[g], partner)

    def activate(g):
        arrived(pre_in.at[g], pre_send.at[g], pre_recv.at[g])
        pre = acc[g] + pre_in[g]
        tanh_val = jnp.tanh(gelu_coef * (pre + gelu_cube * pre * pre * pre))
        inner = gelu_coef * (1.0 + 3.0 * gelu_cube * pre * pre)
        slope = 0.5 * (1.0 + tanh_val) + 0.5 * pre * (1.0 - tanh_val * tanh_val) * inner
        slope *= cot_t[:, g].reshape(units, 2 * half).astype(jnp.float32)
        act_t[:, g] = slope.astype(jnp.bfloat16).reshape(8, ROWS, 2 * half)
        hid_t[:, g] = (0.5 * pre * (1.0 + tanh_val)).reshape(8, ROWS, 2 * half)

    def rs(g, o, msg, src, dst, to):
        send(src, dst, rs_send.at[3 * g + o, msg], rs_recv.at[3 * g + o, msg], to)

    def rs_wait(g, o, msg, dst):
        arrived(dst, rs_send.at[3 * g + o, msg], rs_recv.at[3 * g + o, msg])

    def add(dst, *values):
        total = values[0][...].astype(jnp.float32)
        for value in values[1:]:
            total += value[...].astype(jnp.float32)
        dst[...] = total.astype(dst.dtype)

    def term(g, i):
        upper = lax.rem(me["y"] // 2 + (1 if i < 2 else 0), 2)

        for step in (2, -sign) if i % 2 == 0 else (sign, 0):
            z = wrap(me["z"] + step)
            value = jnp.dot(act_t[:, g].reshape(units, 2 * half), tok[2 * z + upper], preferred_element_type=jnp.float32)
            terms[z, pl.ds(2 * upper, 2), :, pl.ds(g * ROWS, ROWS), :] = value.astype(jnp.bfloat16).reshape(
                2, 4, ROWS, width
            )

    def rs_far(g, o, far):
        hop = cut(hop_a[o].at[g, far], g, o)
        rs(g, o, 3 * far, block(terms, g, o, rows(o, far, 2)), hop, near(ORDERS[o][2], sign))

    def rs_back(g, o, far):
        hop = cut(hop_c[o].at[g, far], g, o)
        rs(g, o, 3 * far + 2, block(terms, g, o, rows(o, far, -sign)), hop, near(ORDERS[o][2], -sign))

    def add_pair(g, o, far, into_hop, plane, *hops):
        one, two, three = ORDERS[o]
        upper = me[two] // 2
        first = 2 * (1 - upper if far else upper)

        def step(i, carry):
            here = block(terms, g, o, {one: line, two: first + i, three: wrap(me[three] + plane)})
            views = [cut(hop.at[g, far, :, i] if o == 2 else hop.at[g, far, i], g, o) for hop in hops]
            add(views[0] if into_hop else here, here, *views)
            return carry

        lax.fori_loop(0, 2, step, 0)

    def rs_cube_on(g, o, far):
        hop = cut(hop_a[o].at[g, far], g, o)
        rs_wait(g, o, 3 * far, hop)
        add_pair(g, o, far, True, sign, hop_a[o])
        rs(g, o, 3 * far + 1, hop, cut(hop_b[o].at[g, far], g, o), near(ORDERS[o][2], sign))

    def rs_plane(g, o, far):
        rs_wait(g, o, 3 * far + 1, cut(hop_b[o].at[g, far], g, o))
        rs_wait(g, o, 3 * far + 2, cut(hop_c[o].at[g, far], g, o))
        add_pair(g, o, far, False, 0, hop_b[o], hop_c[o])
        two = ORDERS[o][1]
        if far:
            rs(g, o, 6, block(terms, g, o, row(o, 2)), cut(row_a.at[g, o], g, o), near(two, 2 if RS_DIRECT[g] else sign))
        else:
            rs(g, o, 8, block(terms, g, o, row(o, -sign)), cut(row_c.at[g, o], g, o), near(two, -sign))
            if RS_DIRECT[g]:
                rs(g, o, 7, block(terms, g, o, row(o, sign)), cut(row_b.at[g, o], g, o), near(two, sign))

    def rs_plane_on(g, o):
        here = cut(row_a.at[g, o], g, o)
        rs_wait(g, o, 6, here)
        add(here, here, block(terms, g, o, row(o, sign)))
        rs(g, o, 7, here, cut(row_b.at[g, o], g, o), near(ORDERS[o][1], sign))

    def rs_line(g, o):
        from_back, from_ahead = cut(row_b.at[g, o], g, o), cut(row_c.at[g, o], g, o)
        rs_wait(g, o, 7, from_back)
        rs_wait(g, o, 8, from_ahead)
        here = block(terms, g, o, row(o, 0))
        if RS_DIRECT[g]:
            across = cut(row_a.at[g, o], g, o)
            rs_wait(g, o, 6, across)
            add(here, here, from_back, from_ahead, across)
        else:
            add(here, here, from_back, from_ahead)
        one = ORDERS[o][0]
        for i, step in enumerate((2, 1, 3)):
            rs(
                g, o, 9 + i, block(terms, g, o, {**me, one: wrap(me[one] + step)}),
                cut(last_in.at[g, o, i], g, o), near(one, step),
            )

    def rs_end(g, o):
        views = [cut(last_in.at[g, o, i], g, o) for i in range(3)]
        for i, view in enumerate(views):
            rs_wait(g, o, 9 + i, view)
        first, count = columns(g, o)
        add(out_grad.at[pl.ds(g * ROWS, ROWS), pl.ds(first, count)], block(terms, g, o, me), *views)

    def act_turn(which):
        @pl.when(core == which)
        def _():
            act[...] = act_t[...].reshape(GROUPS * units, 2 * half).astype(jnp.float32).T.astype(jnp.bfloat16)

    def hidden_turn():
        out_hidden[...] = hid_t[:, :, :, mine].reshape(GROUPS * units, half).T.astype(jnp.bfloat16)

    def input_copy(k):
        return pltpu.make_async_remote_copy(
            src_ref=stage.at[k], dst_ref=out_input.at[:, columns_of(k, core)], send_sem=in_send.at[k],
            recv_sem=in_recv.at[k], device_id=partner, device_id_type=MESH,
        )

    def input_chunks(i, which):
        @pl.when(core == which)
        def _():
            for k in (2 * i, 2 * i + 1):
                weight = weights[k // 2, pl.ds(2 * (k % 2), 2)].reshape(GROUPS * units, width)
                stage[k] = jnp.dot(act[theirs, :], weight, preferred_element_type=jnp.float32).astype(jnp.bfloat16)
                input_copy(k).start()
                out_input[:, columns_of(k, core)] = jnp.dot(
                    act[mine, :], weight, preferred_element_type=jnp.float32
                ).astype(jnp.bfloat16)

    steps = (
        ag_line, ag_plane, ag_plane_on, ag_cube, ag_cube_on, tokens_out, tokens_in, cot_turn, forward, partial_out,
        activate, term, rs_far, rs_back, rs_cube_on, rs_plane, rs_plane_on, rs_line, rs_end, act_turn, input_chunks,
        hidden_turn,
    )
    def drain(keep):
        while len(sent) > keep:
            sent.pop(0).wait_send()

    for name, *where in SCHEDULE:
        if name in (RS_PLANE, RS_LINE, RS_END) and where[0] == GROUPS - 1:
            drain(24)
        steps[name](*where)
    for k in range(8):
        arrived(out_input.at[:, columns_of(k, 1 - core)], in_send.at[k], in_recv.at[k])
        input_copy(k).wait_send()
    drain(0)


def update(
    blocks, total, hidden, input_grad, master, moment_one, moment_two,
    out_hidden, out_input, out_grad, out_master, out_one, out_two, old, new, in_sem, out_sem,
):
    loads = [
        pltpu.make_async_copy(value, old.at[i], in_sem.at[i]) for i, value in enumerate((moment_one, moment_two, master))
    ]
    for copy in loads:
        copy.start()
    rows = input_grad.shape[0] // 4
    copies = [
        pltpu.make_async_copy(
            input_grad.at[pl.ds(i * rows, rows)], out_input.at[pl.ds(i * rows, rows)], out_sem.at[i]
        )
        for i in range(4)
    ]
    copies.append(pltpu.make_async_copy(hidden, out_hidden, out_sem.at[4]))
    for copy in copies:
        copy.start()

    def store(i, value, out):
        new[i] = value
        copies.append(pltpu.make_async_copy(new.at[i], out, out_sem.at[5 + i]))
        copies[-1].start()

    gradient = total[...] / blocks
    store(0, gradient, out_grad)
    loads[0].wait()
    moment_one_new = beta_one * old[0] + (1.0 - beta_one) * gradient
    store(1, moment_one_new, out_one)
    loads[1].wait()
    moment_two_new = beta_two * old[1] + (1.0 - beta_two) * gradient * gradient
    store(2, moment_two_new, out_two)
    loads[2].wait()
    first_fix = 1.0 - beta_one**STEP
    second_fix = 1.0 - beta_two**STEP
    step = learn_rate * (moment_one_new / first_fix) / (jnp.sqrt(moment_two_new / second_fix) + adam_eps)
    store(3, old[2] - step, out_master)
    for copy in copies:
        copy.wait()


def shards(tokens, cotangent, master, moment_one, moment_two):
    half, model = tokens.shape
    units, width = master.shape
    all_units = cotangent.shape[1]
    bf, f32 = jnp.bfloat16, jnp.float32
    dma = pltpu.SemaphoreType.DMA
    vmem, anywhere = pl.BlockSpec(memory_space=pltpu.VMEM), pl.BlockSpec(memory_space=pl.ANY)
    total, hidden, input_grad = pl.pallas_call(
        kernel,
        out_shape=(
            pltpu.VMEM((units, width), f32),
            pltpu.VMEM((half, all_units), bf),
            pltpu.VMEM((half, model), bf),
        ),
        in_specs=[anywhere] * 3,
        out_specs=(vmem, vmem, vmem),
        scratch_shapes=[
            pltpu.VMEM((4, 4, 4, units, width), bf),
            pltpu.VMEM((8, 2 * half, width), bf),
            pltpu.VMEM((4, 4, 4, units, width), bf),
            pltpu.VMEM((GROUPS, 8 * ROWS, 2 * half), f32),
            pltpu.VMEM((GROUPS, 8 * ROWS, 2 * half), f32),
            pltpu.VMEM((8, GROUPS, ROWS, 2 * half), bf),
            pltpu.VMEM((2 * half, all_units), bf),
            pltpu.VMEM((8, GROUPS, ROWS, 2 * half), bf),
            pltpu.VMEM((8, GROUPS, ROWS, 2 * half), f32),
            pltpu.VMEM((8, half, width), bf),
            pltpu.VMEM((units, width), f32),
            pltpu.VMEM((2, half, all_units), bf),
            *(pltpu.VMEM((GROUPS, 2) + ((4, 2) if o == 2 else (2, 4)) + (ROWS, WIDEST), bf) for _ in "abc" for o in range(3)),
            pltpu.VMEM((GROUPS, 3, 4, ROWS, WIDEST), bf),
            pltpu.VMEM((GROUPS, 3, 4, ROWS, WIDEST), bf),
            pltpu.VMEM((GROUPS, 3, 4, ROWS, WIDEST), bf),
            pltpu.VMEM((GROUPS, 3, 3, ROWS, WIDEST), bf),
            dma((2,)), dma((8,)), dma((8,)), dma((8,)), dma((GROUPS,)), dma((GROUPS,)), dma, dma,
            dma((8,)), dma((8,)),
            dma((3 * GROUPS, 12)), dma((3 * GROUPS, 12)), dma((3 * GROUPS, 12)), dma((3 * GROUPS, 12)),
        ],
        compiler_params=pltpu.CompilerParams(
            collective_id=0, has_side_effects=True, vmem_limit_bytes=40 * 2**20
        ),
        name="gather_project_scatter",
    )(*(pltpu.with_memory_space_constraint(value, pltpu.HBM) for value in (master, tokens, cotangent)))
    state = jax.ShapeDtypeStruct((units, width), f32)
    in_vmem = (pltpu.with_memory_space_constraint(value, pltpu.VMEM) for value in (total, hidden, input_grad))
    return pl.pallas_call(
        functools.partial(update, lax.axis_size("node") * lax.axis_size("local")),
        out_shape=(
            jax.ShapeDtypeStruct((half, all_units), bf),
            jax.ShapeDtypeStruct((half, model), bf),
            state, state, state, state,
        ),
        in_specs=[vmem] * 3 + [anywhere] * 3,
        out_specs=(anywhere,) * 6,
        scratch_shapes=[pltpu.VMEM((3, units, width), f32), pltpu.VMEM((4, units, width), f32), dma((3,)), dma((9,))],
        compiler_params=pltpu.CompilerParams(vmem_limit_bytes=16 * 2**20),
        name="adam_and_store",
    )(*in_vmem, *(pltpu.with_memory_space_constraint(value, pltpu.HBM) for value in (master, moment_one, moment_two)))


def solution(mesh):
    in_specs = (
        P(("node", "local"), None),
        P(("node", "local"), None),
        P("local", "node"),
        P("local", "node"),
        P("local", "node"),
    )
    out_specs = (
        P(("node", "local"), None),
        P(("node", "local"), None),
        P("local", "node"),
        P("local", "node"),
        P("local", "node"),
        P("local", "node"),
    )
    return jax.shard_map(shards, mesh=mesh, in_specs=in_specs, out_specs=out_specs, check_vma=False)
```

```python
import functools

import jax
import jax.numpy as jnp
from jax import lax
from jax.experimental import pallas as pl
from jax.experimental.pallas import tpu as pltpu
from jax.sharding import PartitionSpec as P

MESH = pl.DeviceIdType.MESH
STEP = 10

beta_one = 0.9
beta_two = 0.95
learn_rate = 0.001
adam_eps = 1e-08
gelu_coef = 0.7978845608
gelu_cube = 0.044715

ORDERS = (("x", "y", "z"), ("y", "z", "x"), ("z", "x", "y"))
ROWS = 16
GROUPS = 3
COLUMNS = ((0, 384), (384, 256), (640, 256))
WIDEST = 384
AG_DIRECT = (True, False, False)
RS_DIRECT = (False, False, True)


(
    LINE, PLANE, PLANE_ON, CUBE, CUBE_ON, TOKENS_OUT, TOKENS_IN, COT_TURN, FORWARD, PARTIAL_OUT,
    ACTIVATE, TERM, FAR, BACK, RS_CUBE_ON, RS_PLANE, RS_PLANE_ON, RS_LINE, RS_END, ACT_TURN, INPUT,
    HIDDEN,
) = range(22)
SCHEDULE = (
    (LINE, 0, 2), (LINE, 0, 0), (LINE, 0, 1), (LINE, 1, 1), (LINE, 2, 2), (LINE, 2, 1), (TOKENS_OUT,), (LINE, 2, 0),
    (LINE, 1, 2), (LINE, 1, 0), (COT_TURN,), (PLANE, 0, 2), (PLANE, 0, 1), (PLANE, 0, 0), (PLANE, 2, 1),
    (PLANE, 1, 1), (PLANE, 1, 2), (PLANE, 1, 0), (PLANE, 2, 2), (CUBE, 0, 2, 0), (CUBE, 0, 1, 0), (CUBE, 0, 0, 0),
    (PLANE_ON, 1, 2), (CUBE, 0, 2, 1), (TOKENS_IN, 0), (TOKENS_IN, 1), (CUBE, 0, 1, 1), (PLANE, 2, 0),
    (CUBE, 0, 0, 1), (PLANE_ON, 1, 1), (CUBE, 1, 1, 0), (PLANE_ON, 1, 0), (CUBE_ON, 0, 2, 0), (FORWARD, 0, 0, 0),
    (CUBE_ON, 0, 2, 1), (CUBE_ON, 0, 1, 0), (CUBE, 1, 2, 0), (CUBE, 1, 2, 1), (TOKENS_IN, 2), (CUBE_ON, 0, 0, 0),
    (CUBE_ON, 0, 1, 1), (CUBE_ON, 0, 0, 1), (FORWARD, 0, 0, 1), (CUBE, 1, 0, 0), (CUBE, 1, 0, 1), (TOKENS_IN, 3),
    (PLANE_ON, 2, 0), (CUBE_ON, 1, 1, 0), (FORWARD, 0, 2, 0), (FORWARD, 0, 0, 2), (PLANE_ON, 2, 2), (CUBE, 2, 2, 0),
    (FORWARD, 1, 0, 0), (CUBE, 1, 1, 1), (FORWARD, 0, 2, 1), (FORWARD, 0, 1, 0), (FORWARD, 0, 1, 1),
    (FORWARD, 0, 0, 3), (PARTIAL_OUT, 0), (PLANE_ON, 2, 1), (CUBE, 2, 1, 0), (CUBE, 2, 0, 0), (CUBE_ON, 1, 2, 0),
    (CUBE_ON, 1, 2, 1), (CUBE_ON, 1, 0, 0), (FORWARD, 1, 1, 0), (CUBE, 2, 2, 1), (FORWARD, 1, 2, 0),
    (CUBE_ON, 1, 1, 1), (CUBE_ON, 1, 0, 1), (FORWARD, 1, 0, 1), (CUBE, 2, 0, 1), (ACTIVATE, 0), (TERM, 0, 0),
    (CUBE, 2, 1, 1), (TERM, 0, 1), (FAR, 0, 2, 1), (FAR, 0, 2, 0), (TERM, 0, 2), (TERM, 0, 3), (FAR, 0, 0, 1),
    (FAR, 0, 0, 0), (FAR, 0, 1, 1), (FAR, 0, 1, 0), (BACK, 0, 2, 0), (BACK, 0, 2, 1), (BACK, 0, 1, 0),
    (FORWARD, 1, 0, 2), (FORWARD, 1, 2, 1), (FORWARD, 1, 1, 1), (FORWARD, 1, 0, 3), (PARTIAL_OUT, 1),
    (CUBE_ON, 2, 1, 0), (CUBE_ON, 2, 1, 1), (CUBE_ON, 2, 0, 0), (CUBE_ON, 2, 0, 1), (BACK, 0, 1, 1), (BACK, 0, 0, 0),
    (CUBE_ON, 2, 2, 0), (CUBE_ON, 2, 2, 1), (FORWARD, 2, 2, 0), (FORWARD, 2, 0, 0), (FORWARD, 2, 0, 2),
    (BACK, 0, 0, 1), (RS_CUBE_ON, 0, 2, 1), (RS_CUBE_ON, 0, 1, 1), (FORWARD, 2, 0, 1), (RS_CUBE_ON, 0, 0, 1),
    (RS_CUBE_ON, 0, 1, 0), (ACTIVATE, 1), (TERM, 1, 0), (TERM, 1, 1), (TERM, 1, 2), (FAR, 1, 0, 1), (FAR, 1, 2, 1),
    (TERM, 1, 3), (FAR, 1, 2, 0), (BACK, 1, 2, 1), (BACK, 1, 2, 0), (FAR, 1, 1, 1), (FORWARD, 2, 1, 0),
    (FORWARD, 2, 1, 1), (FAR, 1, 1, 0), (FORWARD, 2, 0, 3), (FORWARD, 2, 2, 1), (PARTIAL_OUT, 2), (BACK, 1, 1, 1),
    (FAR, 1, 0, 0), (BACK, 1, 1, 0), (BACK, 1, 0, 0), (RS_CUBE_ON, 0, 2, 0), (RS_PLANE, 0, 1, 1),
    (RS_CUBE_ON, 1, 2, 1), (RS_CUBE_ON, 1, 2, 0), (RS_CUBE_ON, 1, 1, 1), (RS_CUBE_ON, 0, 0, 0), (RS_PLANE, 0, 0, 1),
    (RS_PLANE, 0, 2, 1), (BACK, 1, 0, 1), (ACTIVATE, 2), (TERM, 2, 0), (TERM, 2, 1), (ACT_TURN, 1), (INPUT, 0, 1),
    (FAR, 2, 2, 1), (RS_CUBE_ON, 1, 1, 0), (FAR, 2, 0, 1), (RS_CUBE_ON, 1, 0, 1), (RS_CUBE_ON, 1, 0, 0), (TERM, 2, 2),
    (FAR, 2, 0, 0), (FAR, 2, 2, 0), (BACK, 2, 0, 0), (TERM, 2, 3), (INPUT, 1, 1), (BACK, 2, 2, 0), (FAR, 2, 1, 1),
    (FAR, 2, 1, 0), (BACK, 2, 2, 1), (RS_PLANE, 1, 2, 1), (BACK, 2, 1, 1), (ACT_TURN, 0), (INPUT, 0, 0),
    (RS_CUBE_ON, 2, 0, 1), (BACK, 2, 0, 1), (BACK, 2, 1, 0), (RS_CUBE_ON, 2, 2, 1), (INPUT, 1, 0),
    (RS_CUBE_ON, 2, 1, 1), (RS_CUBE_ON, 2, 2, 0), (RS_PLANE, 1, 1, 1), (RS_PLANE, 1, 0, 1), (RS_CUBE_ON, 2, 1, 0),
    (RS_PLANE, 0, 2, 0), (RS_PLANE, 0, 0, 0), (RS_PLANE_ON, 0, 0), (RS_CUBE_ON, 2, 0, 0), (RS_PLANE, 0, 1, 0),
    (RS_PLANE_ON, 0, 1), (RS_PLANE_ON, 0, 2), (RS_PLANE, 1, 2, 0), (RS_PLANE_ON, 1, 2), (RS_PLANE, 1, 1, 0),
    (INPUT, 2, 0), (RS_PLANE, 2, 2, 1), (INPUT, 2, 1), (RS_PLANE, 1, 0, 0), (RS_PLANE, 2, 0, 1), (RS_PLANE, 2, 1, 1),
    (RS_PLANE, 2, 2, 0), (RS_PLANE_ON, 1, 1), (RS_PLANE_ON, 1, 0), (RS_PLANE, 2, 0, 0), (RS_PLANE, 2, 1, 0),
    (INPUT, 3, 1), (RS_LINE, 0, 1), (RS_LINE, 0, 2), (RS_LINE, 0, 0), (RS_LINE, 1, 2), (INPUT, 3, 0), (RS_LINE, 1, 1),
    (RS_LINE, 1, 0), (RS_LINE, 2, 2), (RS_LINE, 2, 1), (RS_LINE, 2, 0), (HIDDEN,), (RS_END, 0, 0), (RS_END, 1, 1),
    (RS_END, 0, 2), (RS_END, 0, 1), (RS_END, 1, 2), (RS_END, 2, 1), (RS_END, 2, 2), (RS_END, 1, 0), (RS_END, 2, 0),
)


def wrap(value):
    return lax.rem(value + 4, 4)


def device(at, core):
    node = at["z"] * 4 + (at["y"] // 2) * 2 + core
    local = lax.rem(at["y"], 2) * 4 + at["x"]
    return (node, local)


def kernel(
    master_hbm, tokens, cot_hbm, out_grad, out_hidden, out_input,
    weights, tok, terms, acc, pre_in, act_t, act, cot_t, hid_t, stage, master, cot,
    hop_a0, hop_a1, hop_a2, hop_b0, hop_b1, hop_b2, hop_c0, hop_c1, hop_c2, row_a, row_b, row_c, last_in,
    own_sem, tok_sem, tok_send, tok_recv, pre_send, pre_recv, cot_send, cot_recv, in_send, in_recv,
    ag_send, ag_recv, rs_send, rs_recv,
):
    hop_a, hop_b, hop_c = (hop_a0, hop_a1, hop_a2), (hop_b0, hop_b1, hop_b2), (hop_c0, hop_c1, hop_c2)
    node, local = lax.axis_index("node"), lax.axis_index("local")
    core = lax.rem(node, 2)
    me = {"x": lax.rem(local, 4), "y": lax.rem(node // 2, 2) * 2 + local // 4, "z": node // 4}
    sign = 1 - 2 * core
    own = [
        pltpu.make_async_copy(master_hbm, master, own_sem.at[0]),
        pltpu.make_async_copy(cot_hbm, cot.at[core], own_sem.at[1]),
    ]
    for copy in own:
        copy.start()
    width = master.shape[1]
    half = tokens.shape[0]
    units = 8 * ROWS
    groups, orders = range(GROUPS), range(len(ORDERS))

    def near(dim, step):
        at = dict(me)
        at[dim] = wrap(at[dim] + step)
        return device(at, core)

    partner = device(me, 1 - core)
    around = [near(dim, step) for dim in "xyz" for step in (1, 3, 2)] + [partner]
    barrier = pltpu.get_barrier_semaphore()
    for other in around:
        pl.semaphore_signal(barrier, inc=1, device_id=other, device_id_type=MESH)

    mine = pl.ds(pl.multiple_of(core * half, half), half)
    theirs = pl.ds(pl.multiple_of((1 - core) * half, half), half)

    def columns_of(k, which):
        return pl.ds(pl.multiple_of((2 * k + which) * width, 128), width)

    def chunk(i):
        z = wrap(me["z"] + (0, -sign, sign, 2)[i // 2])
        return 2 * z + i % 2

    def own_tokens(i):
        k = chunk(i)
        return pltpu.make_async_copy(tokens.at[:, columns_of(k, core)], tok.at[k, mine, :], tok_sem.at[k])

    for i in range(8):
        own_tokens(i).start()
    own[0].wait()
    weights[me["z"], me["y"], me["x"]] = master[...].astype(jnp.bfloat16)
    pl.semaphore_wait(barrier, len(around))

    sent = []

    def send(src, dst, send_sem, recv_sem, to):
        copy = pltpu.make_async_remote_copy(
            src_ref=src, dst_ref=dst, send_sem=send_sem, recv_sem=recv_sem, device_id=to, device_id_type=MESH
        )
        copy.start()
        sent.append(copy)

    def arrived(dst, send_sem, recv_sem):
        pltpu.make_async_remote_copy(
            src_ref=dst, dst_ref=dst, send_sem=send_sem, recv_sem=recv_sem, device_id=partner, device_id_type=MESH
        ).wait_recv()

    def columns(g, o):
        return COLUMNS[(o - g) % len(COLUMNS)]

    def block(buf, g, o, place):
        first, count = columns(g, o)
        return buf.at[tuple(place[d] for d in "zyx") + (pl.ds(g * ROWS, ROWS), pl.ds(first, count))]

    def cut(buf, g, o):
        return buf.at[..., pl.ds(0, columns(g, o)[1])]

    line = pl.ds(0, 4)

    def pair(dim, far):
        upper = me[dim] // 2
        return pl.ds(2 * (1 - upper if far else upper), 2)

    def ag(g, o, msg, place, to):
        region = block(weights, g, o, place)
        send(region, region, ag_send.at[3 * g + o, msg], ag_recv.at[3 * g + o, msg], to)

    def ag_wait(g, o, msg, place):
        arrived(block(weights, g, o, place), ag_send.at[3 * g + o, msg], ag_recv.at[3 * g + o, msg])

    def row(o, step):
        one, two, three = ORDERS[o]
        return {one: line, two: wrap(me[two] + step), three: me[three]}

    def rows(o, far, step):
        one, two, three = ORDERS[o]
        return {one: line, two: pair(two, far), three: wrap(me[three] + step)}

    def ag_line(g, o):
        for i, step in enumerate((1, 3, 2)):
            ag(g, o, i, me, near(ORDERS[o][0], step))

    def ag_plane(g, o):
        one, two, three = ORDERS[o]
        for i, step in enumerate((1, 3, 2)):
            ag_wait(g, o, i, {**me, one: wrap(me[one] - step)})
        ag(g, o, 3, row(o, 0), near(two, sign))
        ag(g, o, 4, row(o, 0), near(two, -sign))
        if AG_DIRECT[g]:
            ag(g, o, 5, row(o, 0), near(two, 2))

    def ag_plane_on(g, o):
        ag_wait(g, o, 3, row(o, -sign))
        ag(g, o, 5, row(o, -sign), near(ORDERS[o][1], sign))

    def ag_cube(g, o, far):
        three = ORDERS[o][2]
        if AG_DIRECT[g] and not far:
            ag_wait(g, o, 3, row(o, -sign))
        ag_wait(g, o, 4 + far, row(o, 2 if far else sign))
        ag(g, o, 6 + 3 * far, rows(o, far, 0), near(three, sign))
        ag(g, o, 7 + 3 * far, rows(o, far, 0), near(three, -sign))

    def ag_cube_on(g, o, far):
        ag_wait(g, o, 6 + 3 * far, rows(o, far, -sign))
        ag(g, o, 8 + 3 * far, rows(o, far, -sign), near(ORDERS[o][2], sign))

    def from_front(g, o, far):
        ag_wait(g, o, 7 + 3 * far, rows(o, far, sign))

    def from_across(g, o, far):
        ag_wait(g, o, 8 + 3 * far, rows(o, far, 2))

    def tokens_out():
        send(cot_hbm, cot.at[core], cot_send, cot_recv, partner)
        for i in range(8):
            k = chunk(i)
            send(tokens.at[:, columns_of(k, 1 - core)], tok.at[k, mine, :], tok_send.at[k], tok_recv.at[k], partner)

    def tokens_in(i):
        for j in (2 * i, 2 * i + 1):
            own_tokens(j).wait()
            k = chunk(j)
            arrived(tok.at[k, theirs, :], tok_send.at[k], tok_recv.at[k])

    def cot_turn():
        acc[...] = jnp.zeros_like(acc)
        own[1].wait()
        arrived(cot.at[1 - core], cot_send, cot_recv)
        turned = cot[...].reshape(2 * half, GROUPS * units).astype(jnp.float32).T
        cot_t[...] = turned.astype(jnp.bfloat16).reshape(8, GROUPS, ROWS, 2 * half)

    def forward(g, o, i):
        if (o, i) in ((0, 2), (2, 0)):
            from_front(g, o, 0)
            from_front(g, o, 1)
        if (o, i) in ((0, 3), (2, 1)):
            from_across(g, o, 0)
            from_across(g, o, 1)
        if o == 1:
            from_front(g, o, i)
            from_across(g, o, i)
        first, count = columns(g, o)
        here = pl.ds(first, count)

        total = acc[g]
        for j in range(2 if o == 0 else 4):
            z, upper = j // 2, j % 2
            if o == 0:
                z = wrap(me["z"] + (0, -sign, sign, 2)[i])
            elif o == 1:
                z = lax.rem(me["z"] // 2 + i, 2) * 2 + z
            else:
                z, upper = j, lax.rem(me["y"] // 2 + i, 2)
            part = weights[z, pl.ds(2 * upper, 2), :, pl.ds(g * ROWS, ROWS), here].reshape(units, count)
            total += lax.dot_general(
                part, tok[2 * z + upper, :, here], (((1,), (1,)), ((), ())), preferred_element_type=jnp.float32
            )
        acc[g] = total

    def partial_out(g):
        send(acc.at[g], pre_in.at[g], pre_send.at[g], pre_recv.at[g], partner)

    def activate(g):
        arrived(pre_in.at[g], pre_send.at[g], pre_recv.at[g])
        pre = acc[g] + pre_in[g]
        tanh_val = jnp.tanh(gelu_coef * (pre + gelu_cube * pre * pre * pre))
        inner = gelu_coef * (1.0 + 3.0 * gelu_cube * pre * pre)
        slope = 0.5 * (1.0 + tanh_val) + 0.5 * pre * (1.0 - tanh_val * tanh_val) * inner
        slope *= cot_t[:, g].reshape(units, 2 * half).astype(jnp.float32)
        act_t[:, g] = slope.astype(jnp.bfloat16).reshape(8, ROWS, 2 * half)
        hid_t[:, g] = (0.5 * pre * (1.0 + tanh_val)).reshape(8, ROWS, 2 * half)

    def rs(g, o, msg, src, dst, to):
        send(src, dst, rs_send.at[3 * g + o, msg], rs_recv.at[3 * g + o, msg], to)

    def rs_wait(g, o, msg, dst):
        arrived(dst, rs_send.at[3 * g + o, msg], rs_recv.at[3 * g + o, msg])

    def add(dst, *values):
        total = values[0][...].astype(jnp.float32)
        for value in values[1:]:
            total += value[...].astype(jnp.float32)
        dst[...] = total.astype(dst.dtype)

    def term(g, i):
        upper = lax.rem(me["y"] // 2 + (1 if i < 2 else 0), 2)

        for step in (2, -sign) if i % 2 == 0 else (sign, 0):
            z = wrap(me["z"] + step)
            value = jnp.dot(act_t[:, g].reshape(units, 2 * half), tok[2 * z + upper], preferred_element_type=jnp.float32)
            terms[z, pl.ds(2 * upper, 2), :, pl.ds(g * ROWS, ROWS), :] = value.astype(jnp.bfloat16).reshape(
                2, 4, ROWS, width
            )

    def rs_far(g, o, far):
        hop = cut(hop_a[o].at[g, far], g, o)
        rs(g, o, 3 * far, block(terms, g, o, rows(o, far, 2)), hop, near(ORDERS[o][2], sign))

    def rs_back(g, o, far):
        hop = cut(hop_c[o].at[g, far], g, o)
        rs(g, o, 3 * far + 2, block(terms, g, o, rows(o, far, -sign)), hop, near(ORDERS[o][2], -sign))

    def add_pair(g, o, far, into_hop, plane, *hops):
        one, two, three = ORDERS[o]
        upper = me[two] // 2
        first = 2 * (1 - upper if far else upper)

        def step(i, carry):
            here = block(terms, g, o, {one: line, two: first + i, three: wrap(me[three] + plane)})
            views = [cut(hop.at[g, far, :, i] if o == 2 else hop.at[g, far, i], g, o) for hop in hops]
            add(views[0] if into_hop else here, here, *views)
            return carry

        lax.fori_loop(0, 2, step, 0)

    def rs_cube_on(g, o, far):
        hop = cut(hop_a[o].at[g, far], g, o)
        rs_wait(g, o, 3 * far, hop)
        add_pair(g, o, far, True, sign, hop_a[o])
        rs(g, o, 3 * far + 1, hop, cut(hop_b[o].at[g, far], g, o), near(ORDERS[o][2], sign))

    def rs_plane(g, o, far):
        rs_wait(g, o, 3 * far + 1, cut(hop_b[o].at[g, far], g, o))
        rs_wait(g, o, 3 * far + 2, cut(hop_c[o].at[g, far], g, o))
        add_pair(g, o, far, False, 0, hop_b[o], hop_c[o])
        two = ORDERS[o][1]
        if far:
            rs(g, o, 6, block(terms, g, o, row(o, 2)), cut(row_a.at[g, o], g, o), near(two, 2 if RS_DIRECT[g] else sign))
        else:
            rs(g, o, 8, block(terms, g, o, row(o, -sign)), cut(row_c.at[g, o], g, o), near(two, -sign))
            if RS_DIRECT[g]:
                rs(g, o, 7, block(terms, g, o, row(o, sign)), cut(row_b.at[g, o], g, o), near(two, sign))

    def rs_plane_on(g, o):
        here = cut(row_a.at[g, o], g, o)
        rs_wait(g, o, 6, here)
        add(here, here, block(terms, g, o, row(o, sign)))
        rs(g, o, 7, here, cut(row_b.at[g, o], g, o), near(ORDERS[o][1], sign))

    def rs_line(g, o):
        from_back, from_ahead = cut(row_b.at[g, o], g, o), cut(row_c.at[g, o], g, o)
        rs_wait(g, o, 7, from_back)
        rs_wait(g, o, 8, from_ahead)
        here = block(terms, g, o, row(o, 0))
        if RS_DIRECT[g]:
            across = cut(row_a.at[g, o], g, o)
            rs_wait(g, o, 6, across)
            add(here, here, from_back, from_ahead, across)
        else:
            add(here, here, from_back, from_ahead)
        one = ORDERS[o][0]
        for i, step in enumerate((2, 1, 3)):
            rs(
                g, o, 9 + i, block(terms, g, o, {**me, one: wrap(me[one] + step)}),
                cut(last_in.at[g, o, i], g, o), near(one, step),
            )

    def rs_end(g, o):
        views = [cut(last_in.at[g, o, i], g, o) for i in range(3)]
        for i, view in enumerate(views):
            rs_wait(g, o, 9 + i, view)
        first, count = columns(g, o)
        add(out_grad.at[pl.ds(g * ROWS, ROWS), pl.ds(first, count)], block(terms, g, o, me), *views)

    def act_turn(which):
        @pl.when(core == which)
        def _():
            act[...] = act_t[...].reshape(GROUPS * units, 2 * half).astype(jnp.float32).T.astype(jnp.bfloat16)

    def hidden_turn():
        out_hidden[...] = hid_t[:, :, :, mine].reshape(GROUPS * units, half).T.astype(jnp.bfloat16)

    def input_copy(k):
        return pltpu.make_async_remote_copy(
            src_ref=stage.at[k], dst_ref=out_input.at[:, columns_of(k, core)], send_sem=in_send.at[k],
            recv_sem=in_recv.at[k], device_id=partner, device_id_type=MESH,
        )

    def input_chunks(i, which):
        @pl.when(core == which)
        def _():
            for k in (2 * i, 2 * i + 1):
                weight = weights[k // 2, pl.ds(2 * (k % 2), 2)].reshape(GROUPS * units, width)
                stage[k] = jnp.dot(act[theirs, :], weight, preferred_element_type=jnp.float32).astype(jnp.bfloat16)
                input_copy(k).start()
                out_input[:, columns_of(k, core)] = jnp.dot(
                    act[mine, :], weight, preferred_element_type=jnp.float32
                ).astype(jnp.bfloat16)

    steps = (
        ag_line, ag_plane, ag_plane_on, ag_cube, ag_cube_on, tokens_out, tokens_in, cot_turn, forward, partial_out,
        activate, term, rs_far, rs_back, rs_cube_on, rs_plane, rs_plane_on, rs_line, rs_end, act_turn, input_chunks,
        hidden_turn,
    )
    def drain(keep):
        while len(sent) > keep:
            sent.pop(0).wait_send()

    for name, *where in SCHEDULE:
        if name in (RS_PLANE, RS_LINE, RS_END) and where[0] == GROUPS - 1:
            drain(24)
        steps[name](*where)
    for k in range(8):
        arrived(out_input.at[:, columns_of(k, 1 - core)], in_send.at[k], in_recv.at[k])
        input_copy(k).wait_send()
    drain(0)


def update(
    blocks, total, hidden, input_grad, master, moment_one, moment_two,
    out_hidden, out_input, out_grad, out_master, out_one, out_two, old, new, in_sem, out_sem,
):
    rows = input_grad.shape[0] // 4
    copies = [
        pltpu.make_async_copy(
            input_grad.at[pl.ds(i * rows, rows)], out_input.at[pl.ds(i * rows, rows)], out_sem.at[i]
        )
        for i in range(4)
    ]
    copies.append(pltpu.make_async_copy(hidden, out_hidden, out_sem.at[4]))
    for copy in copies:
        copy.start()
    loads = [
        pltpu.make_async_copy(value, old.at[i], in_sem.at[i]) for i, value in enumerate((moment_one, moment_two, master))
    ]
    for copy in loads:
        copy.start()

    def store(i, value, out):
        new[i] = value
        copies.append(pltpu.make_async_copy(new.at[i], out, out_sem.at[5 + i]))
        copies[-1].start()

    gradient = total[...] / blocks
    store(0, gradient, out_grad)
    loads[0].wait()
    moment_one_new = beta_one * old[0] + (1.0 - beta_one) * gradient
    store(1, moment_one_new, out_one)
    loads[1].wait()
    moment_two_new = beta_two * old[1] + (1.0 - beta_two) * gradient * gradient
    store(2, moment_two_new, out_two)
    loads[2].wait()
    first_fix = 1.0 - beta_one**STEP
    second_fix = 1.0 - beta_two**STEP
    step = learn_rate * (moment_one_new / first_fix) / (jnp.sqrt(moment_two_new / second_fix) + adam_eps)
    store(3, old[2] - step, out_master)
    for copy in copies:
        copy.wait()


def shards(tokens, cotangent, master, moment_one, moment_two):
    half, model = tokens.shape
    units, width = master.shape
    all_units = cotangent.shape[1]
    bf, f32 = jnp.bfloat16, jnp.float32
    dma = pltpu.SemaphoreType.DMA
    vmem, anywhere = pl.BlockSpec(memory_space=pltpu.VMEM), pl.BlockSpec(memory_space=pl.ANY)
    total, hidden, input_grad = pl.pallas_call(
        kernel,
        out_shape=(
            pltpu.VMEM((units, width), f32),
            pltpu.VMEM((half, all_units), bf),
            pltpu.VMEM((half, model), bf),
        ),
        in_specs=[anywhere] * 3,
        out_specs=(vmem, vmem, vmem),
        scratch_shapes=[
            pltpu.VMEM((4, 4, 4, units, width), bf),
            pltpu.VMEM((8, 2 * half, width), bf),
            pltpu.VMEM((4, 4, 4, units, width), bf),
            pltpu.VMEM((GROUPS, 8 * ROWS, 2 * half), f32),
            pltpu.VMEM((GROUPS, 8 * ROWS, 2 * half), f32),
            pltpu.VMEM((8, GROUPS, ROWS, 2 * half), bf),
            pltpu.VMEM((2 * half, all_units), bf),
            pltpu.VMEM((8, GROUPS, ROWS, 2 * half), bf),
            pltpu.VMEM((8, GROUPS, ROWS, 2 * half), f32),
            pltpu.VMEM((8, half, width), bf),
            pltpu.VMEM((units, width), f32),
            pltpu.VMEM((2, half, all_units), bf),
            *(pltpu.VMEM((GROUPS, 2) + ((4, 2) if o == 2 else (2, 4)) + (ROWS, WIDEST), bf) for _ in "abc" for o in range(3)),
            pltpu.VMEM((GROUPS, 3, 4, ROWS, WIDEST), bf),
            pltpu.VMEM((GROUPS, 3, 4, ROWS, WIDEST), bf),
            pltpu.VMEM((GROUPS, 3, 4, ROWS, WIDEST), bf),
            pltpu.VMEM((GROUPS, 3, 3, ROWS, WIDEST), bf),
            dma((2,)), dma((8,)), dma((8,)), dma((8,)), dma((GROUPS,)), dma((GROUPS,)), dma, dma,
            dma((8,)), dma((8,)),
            dma((3 * GROUPS, 12)), dma((3 * GROUPS, 12)), dma((3 * GROUPS, 12)), dma((3 * GROUPS, 12)),
        ],
        compiler_params=pltpu.CompilerParams(
            collective_id=0, has_side_effects=True, vmem_limit_bytes=40 * 2**20
        ),
        name="gather_project_scatter",
    )(*(pltpu.with_memory_space_constraint(value, pltpu.HBM) for value in (master, tokens, cotangent)))
    state = jax.ShapeDtypeStruct((units, width), f32)
    in_vmem = (pltpu.with_memory_space_constraint(value, pltpu.VMEM) for value in (total, hidden, input_grad))
    return pl.pallas_call(
        functools.partial(update, lax.axis_size("node") * lax.axis_size("local")),
        out_shape=(
            jax.ShapeDtypeStruct((half, all_units), bf),
            jax.ShapeDtypeStruct((half, model), bf),
            state, state, state, state,
        ),
        in_specs=[vmem] * 3 + [anywhere] * 3,
        out_specs=(anywhere,) * 6,
        scratch_shapes=[pltpu.VMEM((3, units, width), f32), pltpu.VMEM((4, units, width), f32), dma((3,)), dma((9,))],
        compiler_params=pltpu.CompilerParams(vmem_limit_bytes=16 * 2**20),
        name="adam_and_store",
    )(*in_vmem, *(pltpu.with_memory_space_constraint(value, pltpu.HBM) for value in (master, moment_one, moment_two)))


def solution(mesh):
    in_specs = (
        P(("node", "local"), None),
        P(("node", "local"), None),
        P("local", "node"),
        P("local", "node"),
        P("local", "node"),
    )
    out_specs = (
        P(("node", "local"), None),
        P(("node", "local"), None),
        P("local", "node"),
        P("local", "node"),
        P("local", "node"),
        P("local", "node"),
    )
    return jax.shard_map(shards, mesh=mesh, in_specs=in_specs, out_specs=out_specs, check_vma=False)
```
